768 devices in a mesh: stretch: 128 (over x, z_lo, y), col: 6 (over z_hi, core).
Axes of the slice: x: 4, y: 8, z: 12 (z_hi: 3, z_lo: 4; z = z_hi * 4 + z_lo), core: 2. Of those that a mesh axis runs over, the one named last changes fastest.
Arguments:
- queries: bfloat16 [16384, 1536], P('stretch', 'col'), may hold values from -32 to 32
- keys: bfloat16 [16384, 1536], P('stretch', 'col'), may hold values from -32 to 32
- values: bfloat16 [16384, 1536], P('stretch', 'col'), may hold values from -6 to 6
- memory_first: bfloat16 [12, 128, 256], P('col'), may hold values from -0.5 to 0.5
- memory_second_weight: bfloat16 [12, 256, 128], P('col'), may hold values from -0.375 to 0.375
- out_weight: bfloat16 [1536, 2048], P('col'), may hold values from -0.15625 to 0.15625
- decay: float32 [128, 12, 256], P('stretch', 'col'), may hold values from 0.05 to 1
- boundary: int32 [128], P('stretch'), may hold values from 0 to 1
- win_blocks: int32 [12], P('col'), may hold values from 1 to 4
Outputs:
- attention_out: bfloat16 [16384, 1536], P('stretch', 'col')
- memory_out: bfloat16 [16384, 2048], P('stretch')
The draws below stay inside these ranges and needn't reach their ends.
All inputs are finite; a program needn't handle non-finite values.
Results may differ from the reference program's by a relative error of at most 0.017.
Values may be sent and summed in bfloat16 or wider, within the bound.
A program may use at most 192 MiB of HBM per device.

```python
import math
import jax
import jax.numpy as jnp
from jax import lax

D = 2048
HD = 128
MEM_HID = 256
HEADS_DEV = 2
HEADS = 12
TOK_DEV = 128
WMAX = 4
SEQUENCE_BLOCKS = 128
TOKENS = 16384
N_COL = 6


def query_key_pair(key):
    width = HEADS * HD
    base_q = jax.random.truncated_normal(jax.random.fold_in(key, 11), -6.0, 6.0, (TOKENS, width), jnp.float32)
    base_k = jax.random.truncated_normal(jax.random.fold_in(key, 12), -6.0, 6.0, (TOKENS, width), jnp.float32)
    return (base_q, base_k)


def draw_queries(key, part):
    return query_key_pair(key)[0].astype(jnp.bfloat16)


def draw_keys(key, part):
    return query_key_pair(key)[1].astype(jnp.bfloat16)


def draw_decay(key, part):
    units = HEADS * MEM_HID
    share = 0.5
    slow = jax.random.uniform(jax.random.fold_in(key, 21), (units,)) < share
    rate = jnp.exp(jax.random.uniform(jax.random.fold_in(key, 22), (units,), jnp.float32, math.log(0.1), 0.0))
    jitter = jnp.exp(jax.random.uniform(jax.random.fold_in(key, 23), (SEQUENCE_BLOCKS, units), jnp.float32, math.log(0.5), math.log(2.0)))
    gradual_retention = jnp.exp(-rate[None, :] * jitter / SEQUENCE_BLOCKS)
    surprise_values = jax.random.randint(jax.random.fold_in(key, 24), (3,), 0, SEQUENCE_BLOCKS)
    surprise_hit = jnp.any(jnp.arange(SEQUENCE_BLOCKS)[:, None] == surprise_values[None, :], axis=1)
    decay_factor = jax.random.uniform(jax.random.fold_in(key, 25), (SEQUENCE_BLOCKS, units), jnp.float32, 0.65, 0.85)
    gradual_retention = jnp.where(surprise_hit[:, None], gradual_retention * decay_factor, gradual_retention)
    fast_keep = jax.random.uniform(jax.random.fold_in(key, 26), (SEQUENCE_BLOCKS, units), jnp.float32, 0.05, 0.4)
    result = jnp.where(slow[None, :], gradual_retention, fast_keep)
    return result.reshape(SEQUENCE_BLOCKS, HEADS, MEM_HID).astype(jnp.float32)


def draw_boundary(key, part):
    starts = jnp.zeros((SEQUENCE_BLOCKS,), jnp.int32).at[0].set(1)
    later = jax.random.randint(jax.random.fold_in(key, 31), (), SEQUENCE_BLOCKS // 2, SEQUENCE_BLOCKS)
    return starts.at[later].set(1)


def draw_win_blocks(key, part):
    spans = jax.random.randint(jax.random.fold_in(key, 41), (HEADS,), 1, WMAX + 1)
    widest = jax.random.randint(jax.random.fold_in(key, 42), (), 0, HEADS)
    return spans.at[widest].set(WMAX).astype(jnp.int32)


def steps_of(stream_key, shape, split, smallest, high):
    loudness, own = 1.0, jax.random.fold_in(stream_key, 6)
    for dim, blocks in split:
        steps = jnp.exp(jax.random.uniform(jax.random.fold_in(own, dim), (blocks,), jnp.float32, smallest / len(split), high / len(split)))
        loudness = loudness * jnp.repeat(steps, shape[dim] // blocks).reshape([-1 if axis == dim else 1 for axis in range(len(shape))])
    return loudness


def gaussian(rng, extent, scale, most, shards=(), kind=jnp.bfloat16):
    values = jax.random.normal(rng, extent, jnp.float32) * scale
    if len(shards) > 0:
        values = steps_of(rng, extent, shards, -0.22, 0.18) * values
    return jnp.clip(values, min=-most, max=most).astype(kind)


def setup_inputs(seed: int = 0) -> dict:
    seeds = jax.random.split(jax.random.key(seed), 10)
    return {
        "queries": draw_queries(jax.random.fold_in(seeds[9], 71), 0),
        "keys": draw_keys(jax.random.fold_in(seeds[9], 71), 0),
        "values": gaussian(seeds[2], (TOKENS, HEADS * HD), 1.0, 6.0, ((0, 128), (1, 6))),
        "memory_first": gaussian(seeds[3], (HEADS, HD, MEM_HID), HD ** -0.5, 0.5, ((0, 6),)),
        "memory_second_weight": gaussian(seeds[4], (HEADS, MEM_HID, HD), MEM_HID ** -0.5, 0.375, ((0, 6),)),
        "out_weight": gaussian(seeds[5], (HEADS * HD, D), (HEADS * HD) ** -0.5, 0.15625, ((0, 6),)),
        "decay": draw_decay(jax.random.fold_in(seeds[9], 71), 0),
        "boundary": draw_boundary(jax.random.fold_in(seeds[9], 71), 0),
        "win_blocks": draw_win_blocks(jax.random.fold_in(seeds[9], 71), 0),
    }


def silu_slope(z):
    sig = jax.nn.sigmoid(z)
    return sig * (1.0 + z * (1.0 - sig))

def grouped_sum(act, weight):
    group = HEADS_DEV * HD
    left = act.reshape(act.shape[0], N_COL, group).astype(jnp.float32)
    right = weight.reshape(N_COL, group, D).astype(jnp.float32)
    parts = jnp.einsum('tgm,gmd->gtd', left, right, precision=lax.Precision.HIGHEST)
    rounded = lax.optimization_barrier(parts.astype(jnp.bfloat16))
    return lax.optimization_barrier(jnp.sum(rounded.astype(jnp.float32), axis=0))

def attention_all(queries, keys, values, boundary, win_blocks):
    width = HEADS * HD
    span = (WMAX + 1) * TOK_DEV
    seg = jnp.cumsum(boundary).astype(jnp.int32)
    seg_pad = jnp.concatenate([jnp.full((WMAX,), -1, jnp.int32), seg])
    pad_rows = jnp.zeros((WMAX * TOK_DEV, width), jnp.bfloat16)
    key_pad = jnp.concatenate([pad_rows, keys], 0)
    value_pad = jnp.concatenate([pad_rows, values], 0)
    local = jnp.arange(span, dtype=jnp.int32)

    def attend_block(block):
        q_rows = lax.dynamic_slice_in_dim(queries, (block * TOK_DEV).astype(jnp.int32), TOK_DEV, 0)
        k_rows = lax.dynamic_slice_in_dim(key_pad, (block * TOK_DEV).astype(jnp.int32), span, 0)
        v_rows = lax.dynamic_slice_in_dim(value_pad, (block * TOK_DEV).astype(jnp.int32), span, 0)
        key_block = block - WMAX + local // TOK_DEV
        seg_keys = jnp.take(seg_pad, block + local // TOK_DEV)
        same = (key_block >= 0) & (seg_keys == seg[block])
        within = (block - key_block)[None, :] <= win_blocks[:, None]
        key_pos = key_block * TOK_DEV + local % TOK_DEV
        query_pos = block * TOK_DEV + jnp.arange(TOK_DEV, dtype=jnp.int32)
        causal = key_pos[None, :] <= query_pos[:, None]
        mask = (same[None, :] & within)[:, None, :] & causal[None, :, :]
        q3 = q_rows.reshape(TOK_DEV, HEADS, HD).astype(jnp.float32)
        k3 = k_rows.reshape(span, HEADS, HD).astype(jnp.float32)
        v3 = v_rows.reshape(span, HEADS, HD).astype(jnp.float32)
        scores = jnp.einsum('qhd,khd->hqk', q3, k3, precision=lax.Precision.HIGHEST) * (1.0 / math.sqrt(HD))
        scores = jnp.where(mask, scores, -1e+30)
        top = lax.optimization_barrier(jnp.max(scores, axis=-1, keepdims=True))
        expo = jnp.exp(scores - top)
        weights = (expo / lax.optimization_barrier(jnp.sum(expo, axis=-1, keepdims=True))).astype(jnp.bfloat16)
        out = jnp.einsum('hqk,khd->qhd', weights.astype(jnp.float32), v3, precision=lax.Precision.HIGHEST)
        return out.astype(jnp.bfloat16).reshape(TOK_DEV, width)
    blocks_out = lax.map(attend_block, jnp.arange(SEQUENCE_BLOCKS, dtype=jnp.int32))
    return blocks_out.reshape(TOKENS, width)

def reference(queries, keys, values, memory_first, memory_second_weight, out_weight, decay, boundary, win_blocks):
    attention_out = attention_all(queries, keys, values, boundary, win_blocks)
    eta = 1.0 / (TOK_DEV * math.sqrt(SEQUENCE_BLOCKS))
    first_f = memory_first.astype(jnp.float32)
    second_layer_update = memory_second_weight.astype(jnp.float32)
    highest_precision = lax.Precision.HIGHEST

    def advance(carry, inputs):
        state_first, state_second = carry
        q_rows, k_rows, v_rows, decay_row, flag = inputs
        q3 = q_rows.reshape(TOK_DEV, HEADS, HD).astype(jnp.float32)
        k3 = k_rows.reshape(TOK_DEV, HEADS, HD).astype(jnp.float32)
        v3 = v_rows.reshape(TOK_DEV, HEADS, HD).astype(jnp.float32)
        z = jnp.einsum('thd,hdm->htm', k3, first_f, precision=highest_precision)
        hidden_units = jax.nn.silu(z).astype(jnp.bfloat16)
        memory_prediction = jnp.einsum('pof,pfk->opk', hidden_units.astype(jnp.float32), second_layer_update, precision=highest_precision)
        error_signal = (memory_prediction - v3).astype(jnp.bfloat16)
        error_first_layer = error_signal.astype(jnp.float32)
        gradient_second_layer = jnp.einsum('qzu,zqs->qus', hidden_units.astype(jnp.float32), error_first_layer, precision=highest_precision)
        backward_pass = jnp.einsum('lun,uon->ulo', error_first_layer, second_layer_update, precision=highest_precision)
        dz = (backward_pass * silu_slope(z)).astype(jnp.bfloat16)
        grad_first = jnp.einsum('thd,htm->hdm', k3, dz.astype(jnp.float32), precision=highest_precision)
        keep = decay_row * (1 - flag).astype(jnp.float32)
        state_first = state_first * keep[:, None, :] - eta * grad_first
        state_second = state_second * keep[:, :, None] - eta * gradient_second_layer
        fast_first = (first_f + state_first).astype(jnp.bfloat16)
        quick_second_layer = (second_layer_update + state_second).astype(jnp.bfloat16)
        memory_recall = jax.nn.silu(jnp.einsum('thd,hdm->thm', q3, fast_first.astype(jnp.float32), precision=highest_precision)).astype(jnp.bfloat16)
        memory_readout = jnp.einsum('flp,lpe->fle', memory_recall.astype(jnp.float32), quick_second_layer.astype(jnp.float32), precision=highest_precision).astype(jnp.bfloat16)
        out = grouped_sum(memory_readout.reshape(TOK_DEV, HEADS * HD), out_weight).astype(jnp.bfloat16)
        return ((state_first, state_second), out)
    start = (jnp.zeros((HEADS, HD, MEM_HID), jnp.float32), jnp.zeros((HEADS, MEM_HID, HD), jnp.float32))
    width = HEADS * HD
    inputs = (queries.reshape(SEQUENCE_BLOCKS, TOK_DEV, width), keys.reshape(SEQUENCE_BLOCKS, TOK_DEV, width), values.reshape(SEQUENCE_BLOCKS, TOK_DEV, width), decay, boundary)
    carry_end, outs = lax.scan(advance, start, inputs)
    memory_out = outs.reshape(TOKENS, D)
    return (attention_out, memory_out)
```

```python
import functools
import math

import jax
import jax.numpy as jnp
from jax import lax
from jax.experimental import pallas as pl
from jax.experimental.pallas import tpu as pltpu
from jax.sharding import PartitionSpec as P

HD = 128
MEM = 256
WMAX = 4
NY = 8
LANES = 128
SUB = 8
OUT_COLS = 512
MESH = pl.DeviceIdType.MESH
BF16 = jnp.bfloat16
F32 = jnp.float32


def dot(a, b, ca, cb):
    return lax.dot_general(a, b, (((ca,), (cb,)), ((), ())), preferred_element_type=F32)


def kernel(
    n_stretch,
    n_col,
    q_ref,
    k_ref,
    v_ref,
    m1_ref,
    m2_ref,
    wo_ref,
    decay_ref,
    bnd_ref,
    win_ref,
    att_ref,
    out_ref,
    halo,
    keeps,
    upd,
    cut,
    got,
    inner,
    tot,
    rows_in,
    ent,
    ent_in,
    back,
    back_in,
    wall,
    reads,
    part,
    part_in,
    halo_s,
    halo_r,
    keep_s,
    keep_r,
    cut_s,
    cut_r,
    tot_s,
    tot_r,
    ent_s,
    ent_r,
    back_s,
    back_r,
    wall_s,
    wall_r,
    wall_l,
    read_s,
    read_r,
    part_s,
    part_r,
):
    nr = n_stretch // NY
    groups = n_col // 2
    sr = HD // NY
    dh_n = sr // SUB
    tps = 4 * dh_n * 2 // nr
    n_out = out_ref.shape[1] // OUT_COLS

    pos = lax.axis_index("stretch")
    col = lax.axis_index("col")
    y = lax.rem(pos, NY)
    r = pos // NY
    zh = col // 2
    core = lax.rem(col, 2)
    after = lax.rem(pos + 1, n_stretch)
    before = lax.rem(pos + n_stretch - 1, n_stretch)
    sibling = col + 1 - 2 * core

    def at(s, c):
        return {"stretch": s, "col": c}

    def in_row(i):
        return lax.rem(y + i, NY)

    def in_rows(i):
        return lax.rem(r + i, nr)

    def remote(src, dst, send, recv, where):
        return pltpu.make_async_remote_copy(
            src_ref=src, dst_ref=dst, send_sem=send, recv_sem=recv, device_id=where, device_id_type=MESH
        )

    barrier = pltpu.get_barrier_semaphore()

    def greet(where):
        pl.semaphore_signal(barrier, inc=1, device_id=where, device_id_type=MESH)

    for i in range(1, NY):
        greet(at(r * NY + in_row(i), col))
    for i in range(1, nr):
        greet(at(in_rows(i) * NY + y, col))
    greet(at(after, col))
    greet(at(before, col))
    for g in range(1, groups):
        greet(at(pos, lax.rem(col + 2 * g, n_col)))
    greet(at(pos, sibling))
    greeted = (NY - 1) + (nr - 1) + 2 + (groups - 1) + 1

    own_w = pltpu.make_async_copy(wo_ref, wall.at[zh], wall_l)
    own_w.start()
    flag = bnd_ref[0].astype(F32)
    keep2 = decay_ref[0] * (1.0 - flag)
    keeps[y] = jnp.concatenate([keep2, jnp.zeros((SUB - 2, MEM), F32)], 0)
    halo[0, 0:HD, :] = k_ref[...]
    halo[0, HD : 2 * HD, :] = v_ref[...]
    halo[0, 2 * HD :, :] = jnp.full((16, 2 * HD), flag, F32).astype(BF16)

    eta = 1.0 / (HD * math.sqrt(n_stretch))
    for h in range(2):
        cols = slice(h * HD, (h + 1) * HD)
        kh = k_ref[:, cols]
        m2 = m2_ref[h]
        z = dot(kh, m1_ref[h], 1, 0)
        sig = jax.nn.sigmoid(z)
        hidden = (z * sig).astype(BF16)
        err = (dot(hidden, m2, 1, 0) - v_ref[:, cols].astype(F32)).astype(BF16)
        dz = (dot(err, m2, 1, 1) * (sig * (1.0 + z * (1.0 - sig)))).astype(BF16)
        for layer, grad in enumerate((dot(kh, dz, 0, 0), dot(err, hidden, 0, 0))):
            u = -eta * grad
            upd[2 * h + layer] = u
            for s in range(NY):
                cut[s, 2 * h + layer] = u[s * sr : (s + 1) * sr].astype(BF16)
    got[y] = cut[y]

    pl.semaphore_wait(barrier, greeted)

    def keep_copy(i):
        to = in_row(i)
        return remote(keeps.at[y], keeps.at[y], keep_s.at[to], keep_r.at[y], at(r * NY + to, col))

    def cut_copy(i):
        to = in_row(i)
        return remote(cut.at[to], got.at[y], cut_s.at[to], cut_r.at[y], at(r * NY + to, col))

    def halo_copy(k):
        return remote(halo.at[k], halo.at[k + 1], halo_s.at[k], halo_r.at[k + 1], at(after, col))

    def wall_copy(g):
        return remote(wo_ref, wall.at[zh], wall_s.at[g], wall_r.at[zh], at(pos, lax.rem(col + 2 * g, n_col)))

    for i in range(1, NY):
        keep_copy(i).start()
    for i in range(1, NY):
        cut_copy(i).start()
    halo_copy(0).start()
    for g in range(1, groups):
        wall_copy(g).start()

    for i in range(1, NY):
        o = in_row(i)
        remote(keeps.at[o], keeps.at[o], keep_s.at[o], keep_r.at[o], at(pos, col)).wait_recv()
        remote(cut.at[o], got.at[o], cut_s.at[o], cut_r.at[o], at(pos, col)).wait_recv()
    run = [jnp.zeros((sr, MEM), F32) for _ in range(4)]
    decayed = [jnp.ones((1, MEM), F32) for _ in range(2)]
    decayed_at = []
    for b in range(NY):
        decayed_at.append(list(decayed))
        for h in range(2):
            kb = keeps[b, h : h + 1, :]
            for hl in (2 * h, 2 * h + 1):
                inner[b, hl] = run[hl]
                run[hl] = run[hl] * kb + got[b, hl].astype(F32)
            decayed[h] = decayed[h] * kb

    def tiles():
        t = 0
        for hl in range(4):
            for dh in range(dh_n):
                for jh in range(2):
                    yield t // tps, t % tps, hl, slice(dh * SUB, (dh + 1) * SUB), slice(jh * LANES, (jh + 1) * LANES)
                    t += 1

    for owner, slot, hl, ds_, js in tiles():
        tot[owner, slot, 0] = run[hl][ds_, js]
        tot[owner, slot, 1] = jnp.broadcast_to(decayed[hl // 2][:, js], (SUB, LANES))
    rows_in[r] = tot[r]

    def tot_copy(i):
        to = in_rows(i)
        return remote(tot.at[to], rows_in.at[r], tot_s.at[to], tot_r.at[r], at(to * NY + y, col))

    for i in range(1, nr):
        tot_copy(i).start()

    def halo_got(k):
        remote(halo.at[k - 1], halo.at[k], halo_s.at[k - 1], halo_r.at[k], at(pos, col)).wait_recv()

    halo_got(1)
    halo_copy(1).start()

    for i in range(1, nr):
        o = in_rows(i)
        remote(tot.at[o], rows_in.at[o], tot_s.at[o], tot_r.at[o], at(pos, col)).wait_recv()
    for slot in range(tps):
        e = jnp.zeros((SUB, LANES), F32)
        for rr in range(nr):
            ent[rr, slot] = e
            e = e * rows_in[rr, slot, 1] + rows_in[rr, slot, 0]
    ent_in[r] = ent[r]

    def ent_copy(i):
        to = in_rows(i)
        return remote(ent.at[to], ent_in.at[r], ent_s.at[to], ent_r.at[r], at(to * NY + y, col))

    for i in range(1, nr):
        ent_copy(i).start()

    halo_got(2)
    halo_copy(2).start()

    for i in range(1, nr):
        o = in_rows(i)
        remote(ent.at[o], ent_in.at[o], ent_s.at[o], ent_r.at[o], at(pos, col)).wait_recv()
    for owner, slot, hl, ds_, js in tiles():
        e = ent_in[owner, slot]
        for b in range(NY):
            whole = inner[b, hl, ds_, js] + e * decayed_at[b][hl // 2][:, js]
            inner[b, hl, ds_, js] = whole
    for b in range(NY):
        for hl in range(4):
            back[b, hl] = inner[b, hl].astype(BF16)
    back_in[y] = back[y]

    def back_copy(i):
        to = in_row(i)
        return remote(back.at[to], back_in.at[y], back_s.at[to], back_r.at[y], at(r * NY + to, col))

    for i in range(1, NY):
        back_copy(i).start()

    halo_got(3)
    halo_copy(3).start()

    for i in range(1, NY):
        o = in_row(i)
        remote(back.at[o], back_in.at[o], back_s.at[o], back_r.at[o], at(pos, col)).wait_recv()
    read = []
    for h in range(2):
        kh = keep2[h : h + 1, :]
        state = []
        for layer in range(2):
            hl = 2 * h + layer
            entering = jnp.concatenate([back_in[s, hl] for s in range(NY)], 0).astype(F32)
            state.append(entering * kh + upd[hl])
        fast_first = (m1_ref[h].astype(F32) + state[0]).astype(BF16)
        fast_second = (m2_ref[h].astype(F32).T + state[1]).astype(BF16)
        zq = dot(q_ref[:, h * HD : (h + 1) * HD], fast_first, 1, 0)
        recall = (zq * jax.nn.sigmoid(zq)).astype(BF16)
        read.append(dot(recall, fast_second, 1, 1).astype(BF16))
    reads[zh] = jnp.concatenate(read, 1)

    def read_copy(g):
        return remote(
            reads.at[zh], reads.at[zh], read_s.at[g], read_r.at[zh], at(pos, lax.rem(col + 2 * g, n_col))
        )

    for g in range(1, groups):
        read_copy(g).start()

    halo_got(4)
    scale = 1.0 / math.sqrt(HD)
    causal = lax.broadcasted_iota(jnp.int32, (HD, HD), 1) <= lax.broadcasted_iota(jnp.int32, (HD, HD), 0)
    clear = jnp.ones((1, HD), F32)
    clear_at = []
    for k in range(1, WMAX + 1):
        clear = clear * (1.0 - halo[k - 1, 2 * HD : 2 * HD + 16, 0:HD].astype(F32)[0:1])
        clear_at.append(clear * jnp.where(pos >= k, 1.0, 0.0))
    for h in range(2):
        cols = slice(h * HD, (h + 1) * HD)
        qh = q_ref[:, cols]
        s = [jnp.where(causal, dot(qh, halo[0, 0:HD, cols], 1, 1) * scale, -1e30)]
        for k in range(1, WMAX + 1):
            ok = clear_at[k - 1] * jnp.where(win_ref[h] >= k, 1.0, 0.0)
            s.append(jnp.where(ok > 0.5, dot(qh, halo[k, 0:HD, cols], 1, 1) * scale, -1e30))
        s = jnp.concatenate(s, 1)
        top = jnp.max(s, axis=1, keepdims=True)
        e = jnp.exp(s - top)
        w = (e / jnp.sum(e, axis=1, keepdims=True)).astype(BF16)
        vals = jnp.concatenate([halo[k, HD : 2 * HD, cols] for k in range(WMAX + 1)], 0)
        att_ref[:, cols] = dot(w, vals, 1, 0).astype(BF16)

    own_w.wait()
    for g in range(1, groups):
        o = lax.rem(zh + g, groups)
        remote(wo_ref, wall.at[o], wall_s.at[g], wall_r.at[o], at(pos, col)).wait_recv()
        remote(reads.at[o], reads.at[o], read_s.at[g], read_r.at[o], at(pos, col)).wait_recv()
    left = jnp.concatenate([reads[g] for g in range(groups)], 1)

    def part_copy(c):
        return remote(part.at[c], part_in.at[c], part_s.at[c], part_r.at[c], at(pos, sibling))

    for c in range(n_out):
        cs = slice(c * OUT_COLS, (c + 1) * OUT_COLS)
        right = jnp.concatenate([wall[g, :, cs] for g in range(groups)], 0)
        part[c] = dot(left, right, 1, 0).astype(BF16)
        part_copy(c).start()
    for c in range(n_out):
        cs = slice(c * OUT_COLS, (c + 1) * OUT_COLS)
        part_copy(c).wait_recv()
        out_ref[:, cs] = (part[c].astype(F32) + part_in[c].astype(F32)).astype(BF16)

    for i in range(1, NY):
        keep_copy(i).wait_send()
        cut_copy(i).wait_send()
        back_copy(i).wait_send()
    for i in range(1, nr):
        tot_copy(i).wait_send()
        ent_copy(i).wait_send()
    for k in range(WMAX):
        halo_copy(k).wait_send()
    for g in range(1, groups):
        wall_copy(g).wait_send()
        read_copy(g).wait_send()
    for c in range(n_out):
        part_copy(c).wait_send()


def solution(mesh):
    n_stretch, n_col = mesh.shape["stretch"], mesh.shape["col"]
    nr, groups, sr = n_stretch // NY, n_col // 2, HD // NY
    tps = 4 * (sr // SUB) * 2 // nr

    def shards(queries, keys, values, memory_first, memory_second_weight, out_weight, decay, boundary, win_blocks):
        d = out_weight.shape[1]
        vmem = pl.BlockSpec(memory_space=pltpu.VMEM)
        smem = pl.BlockSpec(memory_space=pltpu.SMEM)
        dma = pltpu.SemaphoreType.DMA
        return tuple(
            pl.pallas_call(
                functools.partial(kernel, n_stretch, n_col),
                out_shape=(
                    jax.ShapeDtypeStruct((HD, 2 * HD), BF16),
                    jax.ShapeDtypeStruct((HD, d), BF16),
                ),
                in_specs=[vmem] * 5 + [pl.BlockSpec(memory_space=pl.ANY)] + [vmem, smem, smem],
                out_specs=(vmem, vmem),
                scratch_shapes=[
                    pltpu.VMEM((WMAX + 1, 2 * HD + 16, 2 * HD), BF16),
                    pltpu.VMEM((NY, SUB, MEM), F32),
                    pltpu.VMEM((4, HD, MEM), F32),
                    pltpu.VMEM((NY, 4, sr, MEM), BF16),
                    pltpu.VMEM((NY, 4, sr, MEM), BF16),
                    pltpu.VMEM((NY, 4, sr, MEM), F32),
                    pltpu.VMEM((nr, tps, 2, SUB, LANES), F32),
                    pltpu.VMEM((nr, tps, 2, SUB, LANES), F32),
                    pltpu.VMEM((nr, tps, SUB, LANES), F32),
                    pltpu.VMEM((nr, tps, SUB, LANES), F32),
                    pltpu.VMEM((NY, 4, sr, MEM), BF16),
                    pltpu.VMEM((NY, 4, sr, MEM), BF16),
                    pltpu.VMEM((groups, 2 * HD, d), BF16),
                    pltpu.VMEM((groups, HD, 2 * HD), BF16),
                    pltpu.VMEM((d // OUT_COLS, HD, OUT_COLS), BF16),
                    pltpu.VMEM((d // OUT_COLS, HD, OUT_COLS), BF16),
                    dma((WMAX + 1,)),
                    dma((WMAX + 1,)),
                    dma((NY,)),
                    dma((NY,)),
                    dma((NY,)),
                    dma((NY,)),
                    dma((nr,)),
                    dma((nr,)),
                    dma((nr,)),
                    dma((nr,)),
                    dma((NY,)),
                    dma((NY,)),
                    dma((groups,)),
                    dma((groups,)),
                    dma,
                    dma((groups,)),
                    dma((groups,)),
                    dma((d // OUT_COLS,)),
                    dma((d // OUT_COLS,)),
                ],
                compiler_params=pltpu.CompilerParams(
                    collective_id=0, has_side_effects=True, vmem_limit_bytes=48 * 2**20
                ),
            )(
                queries,
                keys,
                values,
                memory_first,
                memory_second_weight,
                out_weight,
                decay,
                boundary,
                win_blocks,
            )
        )

    placed = (
        P("stretch", "col"),
        P("stretch", "col"),
        P("stretch", "col"),
        P("col", None, None),
        P("col", None, None),
        P("col", None),
        P("stretch", "col", None),
        P("stretch"),
        P("col"),
    )
    return jax.shard_map(
        shards,
        mesh=mesh,
        in_specs=placed,
        out_specs=(P("stretch", "col"), P("stretch", None)),
        check_vma=False,
    )
```

```python
import functools
import math

import jax
import jax.numpy as jnp
from jax import lax
from jax.experimental import pallas as pl
from jax.experimental.pallas import tpu as pltpu
from jax.sharding import PartitionSpec as P

HD = 128
MEM = 256
WMAX = 4
NY = 8
NZ = 4
CHUNKS = 8
LANES = 128
SUB = 8
OUT_COLS = 512
MESH = pl.DeviceIdType.MESH
BF16 = jnp.bfloat16
F32 = jnp.float32


def dot(a, b, ca, cb):
    return lax.dot_general(a, b, (((ca,), (cb,)), ((), ())), preferred_element_type=F32)


def kernel(
    n_stretch,
    n_col,
    q_hbm,
    k_hbm,
    v_hbm,
    m1_hbm,
    m2_hbm,
    wo_ref,
    decay_hbm,
    bnd_ref,
    win_ref,
    att_ref,
    out_ref,
    q_ref,
    m1_ref,
    m2_ref,
    decay_ref,
    halo,
    keeps,
    upd,
    cut,
    got,
    inner,
    tot,
    rows_in,
    ent,
    ent_in,
    back,
    back_in,
    wall,
    reads,
    part,
    part_in,
    in_s,
    halo_s,
    halo_r,
    keep_s,
    keep_r,
    cut_s,
    cut_r,
    tot_s,
    tot_r,
    ent_s,
    ent_r,
    back_s,
    back_r,
    up_s,
    up_r,
    down_s,
    down_r,
    wall_l,
    read_s,
    read_r,
    part_s,
    part_r,
):
    nr = n_stretch // NY
    groups = n_col // 2
    sr = HD // NY
    dh_n = sr // SUB
    tps = 4 * dh_n * 2 // nr
    n_out = out_ref.shape[1] // OUT_COLS

    pos = lax.axis_index("stretch")
    col = lax.axis_index("col")
    y = lax.rem(pos, NY)
    r = pos // NY
    zl = lax.rem(r, NZ)
    zh = col // 2
    core = lax.rem(col, 2)
    after = lax.rem(pos + 1, n_stretch)
    before = lax.rem(pos + n_stretch - 1, n_stretch)
    sibling = col + 1 - 2 * core

    def at(s, c):
        return {"stretch": s, "col": c}

    def in_row(i):
        return lax.rem(y + i, NY)

    def in_rows(i):
        return lax.rem(r + i, nr)

    ends, starts = zl == NZ - 1, zl == 0
    above = at(
        jnp.where(ends, pos - (NZ - 1) * NY, pos + NY), jnp.where(ends, lax.rem(col + 2, n_col), col)
    )
    below = at(
        jnp.where(starts, pos + (NZ - 1) * NY, pos - NY), jnp.where(starts, lax.rem(col + n_col - 2, n_col), col)
    )

    def remote(src, dst, send, recv, where):
        return pltpu.make_async_remote_copy(
            src_ref=src, dst_ref=dst, send_sem=send, recv_sem=recv, device_id=where, device_id_type=MESH
        )

    barrier = pltpu.get_barrier_semaphore()

    def greet(where):
        pl.semaphore_signal(barrier, inc=1, device_id=where, device_id_type=MESH)

    for i in range(1, NY):
        greet(at(r * NY + in_row(i), col))
    for i in range(1, nr):
        greet(at(in_rows(i) * NY + y, col))
    greet(at(after, col))
    greet(at(before, col))
    for g in range(1, groups):
        greet(at(pos, lax.rem(col + 2 * g, n_col)))
    greet(at(pos, sibling))
    greet(above)
    greet(below)
    greeted = (NY - 1) + (nr - 1) + 2 + (groups - 1) + 1 + 2

    own = halo.at[0]
    loads = [
        pltpu.make_async_copy(src, dst, in_s.at[i])
        for i, (src, dst) in enumerate(
            (
                (k_hbm, own.at[0:HD]),
                (m1_hbm, m1_ref),
                (m2_hbm, m2_ref),
                (v_hbm, own.at[HD : 2 * HD]),
                (decay_hbm, decay_ref),
                (q_hbm, q_ref),
            )
        )
    ]
    for load in loads:
        load.start()
    own_w = pltpu.make_async_copy(wo_ref, wall.at[zh], wall_l)
    own_w.start()
    flag = bnd_ref[0].astype(F32)
    halo[0, 2 * HD :, :] = jnp.full((16, 2 * HD), flag, F32).astype(BF16)
    for load in loads:
        load.wait()
    keep2 = decay_ref[0] * (1.0 - flag)
    keeps[y] = jnp.concatenate([keep2, jnp.zeros((SUB - 2, MEM), F32)], 0)

    eta = 1.0 / (HD * math.sqrt(n_stretch))
    for h in range(2):
        cols = slice(h * HD, (h + 1) * HD)
        kh = halo[0, 0:HD, cols]
        m2 = m2_ref[h]
        z = dot(kh, m1_ref[h], 1, 0)
        sig = jax.nn.sigmoid(z)
        hidden = (z * sig).astype(BF16)
        err = (dot(hidden, m2, 1, 0) - halo[0, HD : 2 * HD, cols].astype(F32)).astype(BF16)
        dz = (dot(err, m2, 1, 1) * (sig * (1.0 + z * (1.0 - sig)))).astype(BF16)
        for layer, grad in enumerate((dot(kh, dz, 0, 0), dot(err, hidden, 0, 0))):
            u = -eta * grad
            upd[2 * h + layer] = u
            for s in range(NY):
                cut[s, 2 * h + layer] = u[s * sr : (s + 1) * sr].astype(BF16)
    got[y] = cut[y]

    pl.semaphore_wait(barrier, greeted)

    def keep_copy(i):
        to = in_row(i)
        return remote(keeps.at[y], keeps.at[y], keep_s.at[to], keep_r.at[y], at(r * NY + to, col))

    def cut_copy(i):
        to = in_row(i)
        return remote(cut.at[to], got.at[y], cut_s.at[to], cut_r.at[y], at(r * NY + to, col))

    def halo_copy(k):
        return remote(halo.at[k], halo.at[k + 1], halo_s.at[k], halo_r.at[k + 1], at(after, col))

    rows_c = 2 * HD // CHUNKS
    wait_g = lax.rem(zh + groups - 1, groups), lax.rem(zh + 1, groups)
    send_g = jnp.where(ends, zh, wait_g[0]), jnp.where(starts, zh, wait_g[1])

    def wall_copy(way, g, c):
        piece = wall.at[g, pl.ds(pl.multiple_of(c * rows_c, rows_c), rows_c)]
        sem_s, sem_r = ((up_s, up_r), (down_s, down_r))[way]
        return remote(piece, piece, sem_s.at[c], sem_r.at[c], (above, below)[way])

    def pump(j):
        for way, (d, last) in enumerate(((zl, ends), (NZ - 1 - zl, starts))):
            c = j - d

            @pl.when(jnp.logical_and(jnp.logical_not(last), jnp.logical_and(c >= 0, c < CHUNKS)))
            def _():
                wall_copy(way, wait_g[way], c).wait_recv()
                wall_copy(way, send_g[way], c).start()

    def pump_first():
        for way, last in enumerate((ends, starts)):

            @pl.when(last)
            def _():
                for c in range(CHUNKS):
                    wall_copy(way, send_g[way], c).start()

    def pump_last():
        for way, last in enumerate((ends, starts)):

            @pl.when(last)
            def _():
                for c in range(CHUNKS):
                    wall_copy(way, wait_g[way], c).wait_recv()

    for i in range(1, NY):
        keep_copy(i).start()
    for i in range(1, NY):
        cut_copy(i).start()
    halo_copy(0).start()
    own_w.wait()
    pump_first()
    pump(0)

    for i in range(1, NY):
        o = in_row(i)
        remote(keeps.at[o], keeps.at[o], keep_s.at[o], keep_r.at[o], at(pos, col)).wait_recv()
        remote(cut.at[o], got.at[o], cut_s.at[o], cut_r.at[o], at(pos, col)).wait_recv()
    run = [jnp.zeros((sr, MEM), F32) for _ in range(4)]
    decayed = [jnp.ones((1, MEM), F32) for _ in range(2)]
    decayed_at = []
    for b in range(NY):
        decayed_at.append(list(decayed))
        for h in range(2):
            kb = keeps[b, h : h + 1, :]
            for hl in (2 * h, 2 * h + 1):
                inner[b, hl] = run[hl]
                run[hl] = run[hl] * kb + got[b, hl].astype(F32)
            decayed[h] = decayed[h] * kb

    def tiles():
        t = 0
        for hl in range(4):
            for dh in range(dh_n):
                for jh in range(2):
                    yield t // tps, t % tps, hl, slice(dh * SUB, (dh + 1) * SUB), slice(jh * LANES, (jh + 1) * LANES)
                    t += 1

    for owner, slot, hl, ds_, js in tiles():
        tot[owner, slot, 0] = run[hl][ds_, js]
        tot[owner, slot, 1] = jnp.broadcast_to(decayed[hl // 2][:, js], (SUB, LANES))
    rows_in[r] = tot[r]

    def tot_copy(i):
        to = in_rows(i)
        return remote(tot.at[to], rows_in.at[r], tot_s.at[to], tot_r.at[r], at(to * NY + y, col))

    for i in range(1, nr):
        tot_copy(i).start()

    def halo_got(k):
        remote(halo.at[k - 1], halo.at[k], halo_s.at[k - 1], halo_r.at[k], at(pos, col)).wait_recv()

    pump(1)
    halo_got(1)
    halo_copy(1).start()
    pump(2)

    for i in range(1, nr):
        o = in_rows(i)
        remote(tot.at[o], rows_in.at[o], tot_s.at[o], tot_r.at[o], at(pos, col)).wait_recv()
    for slot in range(tps):
        e = jnp.zeros((SUB, LANES), F32)
        for rr in range(nr):
            ent[rr, slot] = e
            e = e * rows_in[rr, slot, 1] + rows_in[rr, slot, 0]
    ent_in[r] = ent[r]

    def ent_copy(i):
        to = in_rows(i)
        return remote(ent.at[to], ent_in.at[r], ent_s.at[to], ent_r.at[r], at(to * NY + y, col))

    for i in range(1, nr):
        ent_copy(i).start()

    pump(3)
    halo_got(2)
    halo_copy(2).start()
    pump(4)

    for i in range(1, nr):
        o = in_rows(i)
        remote(ent.at[o], ent_in.at[o], ent_s.at[o], ent_r.at[o], at(pos, col)).wait_recv()
    for owner, slot, hl, ds_, js in tiles():
        e = ent_in[owner, slot]
        for b in range(NY):
            whole = inner[b, hl, ds_, js] + e * decayed_at[b][hl // 2][:, js]
            inner[b, hl, ds_, js] = whole
    for b in range(NY):
        for hl in range(4):
            back[b, hl] = inner[b, hl].astype(BF16)
    back_in[y] = back[y]

    def back_copy(i):
        to = in_row(i)
        return remote(back.at[to], back_in.at[y], back_s.at[to], back_r.at[y], at(r * NY + to, col))

    for i in range(1, NY):
        back_copy(i).start()

    pump(5)
    halo_got(3)
    halo_copy(3).start()
    pump(6)

    for i in range(1, NY):
        o = in_row(i)
        remote(back.at[o], back_in.at[o], back_s.at[o], back_r.at[o], at(pos, col)).wait_recv()
    read = []
    for h in range(2):
        kh = keep2[h : h + 1, :]
        state = []
        for layer in range(2):
            hl = 2 * h + layer
            entering = jnp.concatenate([back_in[s, hl] for s in range(NY)], 0).astype(F32)
            state.append(entering * kh + upd[hl])
        fast_first = (m1_ref[h].astype(F32) + state[0]).astype(BF16)
        fast_second = (m2_ref[h].astype(F32).T + state[1]).astype(BF16)
        zq = dot(q_ref[:, h * HD : (h + 1) * HD], fast_first, 1, 0)
        recall = (zq * jax.nn.sigmoid(zq)).astype(BF16)
        read.append(dot(recall, fast_second, 1, 1).astype(BF16))
    reads[zh] = jnp.concatenate(read, 1)

    def read_copy(g):
        return remote(
            reads.at[zh], reads.at[zh], read_s.at[g], read_r.at[zh], at(pos, lax.rem(col + 2 * g, n_col))
        )

    for g in range(1, groups):
        read_copy(g).start()

    pump(7)
    halo_got(4)
    scale = 1.0 / math.sqrt(HD)
    causal = lax.broadcasted_iota(jnp.int32, (HD, HD), 1) <= lax.broadcasted_iota(jnp.int32, (HD, HD), 0)
    clear = jnp.ones((1, HD), F32)
    clear_at = []
    for k in range(1, WMAX + 1):
        clear = clear * (1.0 - halo[k - 1, 2 * HD : 2 * HD + 16, 0:HD].astype(F32)[0:1])
        clear_at.append(clear * jnp.where(pos >= k, 1.0, 0.0))
    for h in range(2):
        cols = slice(h * HD, (h + 1) * HD)
        qh = q_ref[:, cols]
        s = [jnp.where(causal, dot(qh, halo[0, 0:HD, cols], 1, 1) * scale, -1e30)]
        for k in range(1, WMAX + 1):
            ok = clear_at[k - 1] * jnp.where(win_ref[h] >= k, 1.0, 0.0)
            s.append(jnp.where(ok > 0.5, dot(qh, halo[k, 0:HD, cols], 1, 1) * scale, -1e30))
        s = jnp.concatenate(s, 1)
        top = jnp.max(s, axis=1, keepdims=True)
        e = jnp.exp(s - top)
        w = (e / jnp.sum(e, axis=1, keepdims=True)).astype(BF16)
        vals = jnp.concatenate([halo[k, HD : 2 * HD, cols] for k in range(WMAX + 1)], 0)
        att_ref[:, cols] = dot(w, vals, 1, 0).astype(BF16)

    for j in range(8, CHUNKS + NZ - 2):
        pump(j)
    pump_last()
    for g in range(1, groups):
        o = lax.rem(zh + g, groups)
        remote(reads.at[o], reads.at[o], read_s.at[g], read_r.at[o], at(pos, col)).wait_recv()
    left = jnp.concatenate([reads[g] for g in range(groups)], 1)

    def part_copy(c):
        return remote(part.at[c], part_in.at[c], part_s.at[c], part_r.at[c], at(pos, sibling))

    for c in range(n_out):
        cs = slice(c * OUT_COLS, (c + 1) * OUT_COLS)
        right = jnp.concatenate([wall[g, :, cs] for g in range(groups)], 0)
        part[c] = dot(left, right, 1, 0).astype(BF16)
        part_copy(c).start()
    for c in range(n_out):
        cs = slice(c * OUT_COLS, (c + 1) * OUT_COLS)
        part_copy(c).wait_recv()
        out_ref[:, cs] = (part[c].astype(F32) + part_in[c].astype(F32)).astype(BF16)

    for i in range(1, NY):
        keep_copy(i).wait_send()
        cut_copy(i).wait_send()
        back_copy(i).wait_send()
    for i in range(1, nr):
        tot_copy(i).wait_send()
        ent_copy(i).wait_send()
    for k in range(WMAX):
        halo_copy(k).wait_send()
    for g in range(1, groups):
        read_copy(g).wait_send()
    for c in range(CHUNKS):
        for way in range(2):
            wall_copy(way, send_g[way], c).wait_send()
    for c in range(n_out):
        part_copy(c).wait_send()


def solution(mesh):
    n_stretch, n_col = mesh.shape["stretch"], mesh.shape["col"]
    nr, groups, sr = n_stretch // NY, n_col // 2, HD // NY
    tps = 4 * (sr // SUB) * 2 // nr

    def shards(queries, keys, values, memory_first, memory_second_weight, out_weight, decay, boundary, win_blocks):
        d = out_weight.shape[1]
        hbm = pl.BlockSpec(memory_space=pltpu.HBM)
        vmem = pl.BlockSpec(memory_space=pltpu.VMEM)
        smem = pl.BlockSpec(memory_space=pltpu.SMEM)
        dma = pltpu.SemaphoreType.DMA
        return tuple(
            pl.pallas_call(
                functools.partial(kernel, n_stretch, n_col),
                out_shape=(
                    jax.ShapeDtypeStruct((HD, 2 * HD), BF16),
                    jax.ShapeDtypeStruct((HD, d), BF16),
                ),
                in_specs=[hbm] * 7 + [smem] * 2,
                out_specs=(vmem, vmem),
                scratch_shapes=[
                    pltpu.VMEM((HD, 2 * HD), BF16),
                    pltpu.VMEM((2, HD, MEM), BF16),
                    pltpu.VMEM((2, MEM, HD), BF16),
                    pltpu.VMEM((1, 2, MEM), F32),
                    pltpu.VMEM((WMAX + 1, 2 * HD + 16, 2 * HD), BF16),
                    pltpu.VMEM((NY, SUB, MEM), F32),
                    pltpu.VMEM((4, HD, MEM), F32),
                    pltpu.VMEM((NY, 4, sr, MEM), BF16),
                    pltpu.VMEM((NY, 4, sr, MEM), BF16),
                    pltpu.VMEM((NY, 4, sr, MEM), F32),
                    pltpu.VMEM((nr, tps, 2, SUB, LANES), F32),
                    pltpu.VMEM((nr, tps, 2, SUB, LANES), F32),
                    pltpu.VMEM((nr, tps, SUB, LANES), F32),
                    pltpu.VMEM((nr, tps, SUB, LANES), F32),
                    pltpu.VMEM((NY, 4, sr, MEM), BF16),
                    pltpu.VMEM((NY, 4, sr, MEM), BF16),
                    pltpu.VMEM((groups, 2 * HD, d), BF16),
                    pltpu.VMEM((groups, HD, 2 * HD), BF16),
                    pltpu.VMEM((d // OUT_COLS, HD, OUT_COLS), BF16),
                    pltpu.VMEM((d // OUT_COLS, HD, OUT_COLS), BF16),
                    dma((6,)),
                    dma((WMAX + 1,)),
                    dma((WMAX + 1,)),
                    dma((NY,)),
                    dma((NY,)),
                    dma((NY,)),
                    dma((NY,)),
                    dma((nr,)),
                    dma((nr,)),
                    dma((nr,)),
                    dma((nr,)),
                    dma((NY,)),
                    dma((NY,)),
                    dma((CHUNKS,)),
                    dma((CHUNKS,)),
                    dma((CHUNKS,)),
                    dma((CHUNKS,)),
                    dma,
                    dma((groups,)),
                    dma((groups,)),
                    dma((d // OUT_COLS,)),
                    dma((d // OUT_COLS,)),
                ],
                compiler_params=pltpu.CompilerParams(
                    collective_id=0, has_side_effects=True, vmem_limit_bytes=60 * 2**20
                ),
            )(
                queries,
                keys,
                values,
                memory_first,
                memory_second_weight,
                out_weight,
                decay,
                boundary,
                win_blocks,
            )
        )

    placed = (
        P("stretch", "col"),
        P("stretch", "col"),
        P("stretch", "col"),
        P("col", None, None),
        P("col", None, None),
        P("col", None),
        P("stretch", "col", None),
        P("stretch"),
        P("col"),
    )
    return jax.shard_map(
        shards,
        mesh=mesh,
        in_specs=placed,
        out_specs=(P("stretch", "col"), P("stretch", None)),
        check_vma=False,
    )
```

```python
import functools
import math

import jax
import jax.numpy as jnp
from jax import lax
from jax.experimental import pallas as pl
from jax.experimental.pallas import tpu as pltpu
from jax.sharding import PartitionSpec as P

HD = 128
MEM = 256
WMAX = 4
NY = 8
NZ = 4
DIRECT = 128
PARTS = 5
DUE = (((0, 1), (2, 3), (4,), ()), ((0,), (1, 2), (3,), (4,)), ((), (0,), (1, 2), (3, 4)), ((), (), (), ()))
LANES = 128
SUB = 8
OUT_COLS = 512
MESH = pl.DeviceIdType.MESH
BF16 = jnp.bfloat16
F32 = jnp.float32


def dot(a, b, ca, cb):
    return lax.dot_general(a, b, (((ca,), (cb,)), ((), ())), preferred_element_type=F32)


def kernel(
    n_stretch,
    n_col,
    q_hbm,
    k_hbm,
    v_hbm,
    m1_hbm,
    m2_hbm,
    wo_ref,
    decay_hbm,
    win_hbm,
    bnd_ref,
    att_ref,
    out_ref,
    q_ref,
    m1_ref,
    m2_ref,
    decay_ref,
    win_ref,
    halo,
    keeps,
    upd,
    cut,
    got,
    inner,
    tot,
    rows_in,
    ent,
    ent_in,
    back,
    back_in,
    wall,
    reads,
    part,
    part_in,
    in_s,
    halo_s,
    halo_r,
    keep_s,
    keep_r,
    cut_s,
    cut_r,
    tot_s,
    tot_r,
    ent_s,
    ent_r,
    back_s,
    back_r,
    up_s,
    up_r,
    down_s,
    down_r,
    across_s,
    across_r,
    wall_l,
    read_s,
    read_r,
    part_s,
    part_r,
):
    nr = n_stretch // NY
    nx = nr // NZ
    groups = n_col // 2
    sr = HD // NY
    dh_n = sr // SUB
    tps = 4 * dh_n * 2 // nr
    n_out = out_ref.shape[1] // OUT_COLS

    pos = lax.axis_index("stretch")
    col = lax.axis_index("col")
    y = lax.rem(pos, NY)
    r = pos // NY
    zl = lax.rem(r, NZ)
    xs = r // NZ
    zh = col // 2
    core = lax.rem(col, 2)
    after = lax.rem(pos + 1, n_stretch)
    before = lax.rem(pos + n_stretch - 1, n_stretch)
    sibling = col + 1 - 2 * core

    def at(s, c):
        return {"stretch": s, "col": c}

    def in_row(i):
        return lax.rem(y + i, NY)

    def in_rows(i):
        return lax.rem(r + i, nr)

    ends, starts = zl == NZ - 1, zl == 0
    above = at(
        jnp.where(ends, pos - (NZ - 1) * NY, pos + NY), jnp.where(ends, lax.rem(col + 2, n_col), col)
    )
    below = at(
        jnp.where(starts, pos + (NZ - 1) * NY, pos - NY), jnp.where(starts, lax.rem(col + n_col - 2, n_col), col)
    )

    def remote(src, dst, send, recv, where):
        return pltpu.make_async_remote_copy(
            src_ref=src, dst_ref=dst, send_sem=send, recv_sem=recv, device_id=where, device_id_type=MESH
        )

    barrier = pltpu.get_barrier_semaphore()

    def greet(where):
        pl.semaphore_signal(barrier, inc=1, device_id=where, device_id_type=MESH)

    for i in range(1, NY):
        greet(at(r * NY + in_row(i), col))
    for i in range(1, nr):
        greet(at(in_rows(i) * NY + y, col))
    greet(at(after, col))
    greet(at(before, col))
    for g in range(1, groups):
        greet(at(pos, lax.rem(col + 2 * g, n_col)))
    greet(at(pos, sibling))
    greet(above)
    greet(below)
    greeted = (NY - 1) + (nr - 1) + 2 + (groups - 1) + 1 + 2

    own = halo.at[0]
    loads = [
        pltpu.make_async_copy(src, dst, in_s.at[i])
        for i, (src, dst) in enumerate(
            (
                (k_hbm, own.at[0:HD]),
                (m1_hbm, m1_ref),
                (m2_hbm, m2_ref),
                (v_hbm, own.at[HD : 2 * HD]),
                (decay_hbm, decay_ref),
                (q_hbm, q_ref),
                (win_hbm, win_ref),
            )
        )
    ]
    for load in loads:
        load.start()
    own_w = pltpu.make_async_copy(wo_ref, wall.at[zh], wall_l)
    own_w.start()
    for load in loads:
        load.wait()
    flag = bnd_ref[0].astype(F32)
    halo[0, 2 * HD :, :] = jnp.full((16, 2 * HD), flag, F32).astype(BF16)
    keep2 = decay_ref[0] * (1.0 - flag)
    keeps[y] = jnp.concatenate([keep2, jnp.zeros((SUB - 2, MEM), F32)], 0)

    eta = 1.0 / (HD * math.sqrt(n_stretch))
    for h in range(2):
        cols = slice(h * HD, (h + 1) * HD)
        kh = halo[0, 0:HD, cols]
        m2 = m2_ref[h]
        z = dot(kh, m1_ref[h], 1, 0)
        sig = jax.nn.sigmoid(z)
        hidden = (z * sig).astype(BF16)
        err = (dot(hidden, m2, 1, 0) - halo[0, HD : 2 * HD, cols].astype(F32)).astype(BF16)
        dz = (dot(err, m2, 1, 1) * (sig * (1.0 + z * (1.0 - sig)))).astype(BF16)
        for layer, grad in enumerate((dot(kh, dz, 0, 0), dot(err, hidden, 0, 0))):
            u = -eta * grad
            upd[2 * h + layer] = u
            for s in range(NY):
                cut[s, 2 * h + layer] = u[s * sr : (s + 1) * sr].astype(BF16)
    got[y] = cut[y]

    pl.semaphore_wait(barrier, greeted)

    def keep_copy(i):
        to = in_row(i)
        return remote(keeps.at[y], keeps.at[y], keep_s.at[to], keep_r.at[y], at(r * NY + to, col))

    def cut_copy(i):
        to = in_row(i)
        return remote(cut.at[to], got.at[y], cut_s.at[to], cut_r.at[y], at(r * NY + to, col))

    def halo_copy(k):
        return remote(halo.at[k], halo.at[k + 1], halo_s.at[k], halo_r.at[k + 1], at(after, col))

    rows_x = (2 * HD - DIRECT) // nx
    rows_c = DIRECT // (PARTS - 1)
    wait_g = lax.rem(zh + groups - 1, groups), lax.rem(zh + 1, groups)
    send_g = jnp.where(ends, zh, wait_g[0]), jnp.where(starts, zh, wait_g[1])
    chain = zl, NZ - 1 - zl

    def share(g, xx):
        return wall.at[g, pl.ds(pl.multiple_of(DIRECT + xx * rows_x, rows_x), rows_x)]

    def wall_copy(way, g, c):
        piece = share(g, xs) if c == 0 else wall.at[g, (c - 1) * rows_c : c * rows_c]
        sem_s, sem_r = ((up_s, up_r), (down_s, down_r))[way]
        return remote(piece, piece, sem_s.at[c], sem_r.at[c], (above, below)[way])

    def across_copy(way, i):
        piece = share(wait_g[way], xs)
        to = lax.rem(pos + i * NY * NZ, n_stretch)
        return remote(piece, piece, across_s.at[way, i], across_r.at[way, i], at(to, col))

    def across_got(way, i):
        piece = share(wait_g[way], lax.rem(xs + nx - i, nx))
        remote(piece, piece, across_s.at[way, i], across_r.at[way, i], at(pos, col)).wait_recv()

    def took(way, c):
        wall_copy(way, wait_g[way], c).wait_recv()
        if c == 0:
            for i in range(1, nx):
                across_copy(way, i).start()

    def pump(point):
        for way in range(2):
            for d in range(NZ - 1):

                @pl.when(chain[way] == d)
                def _():
                    for c in DUE[d][point]:
                        took(way, c)
                        wall_copy(way, send_g[way], c).start()

            if point == 2:

                @pl.when(chain[way] == NZ - 1)
                def _():
                    took(way, 0)

    def pump_first():
        for c in range(PARTS):
            for way in range(2):

                @pl.when(chain[way] == NZ - 1)
                def _():
                    wall_copy(way, zh, c).start()

    def pump_last():
        for way in range(2):

            @pl.when(chain[way] == NZ - 1)
            def _():
                for c in range(1, PARTS):
                    took(way, c)

            for i in range(1, nx):
                across_got(way, i)

    for i in range(1, NY):
        keep_copy(i).start()
    for i in range(1, NY):
        cut_copy(i).start()
    own_w.wait()
    pump_first()
    pump(0)

    for i in range(1, NY):
        o = in_row(i)
        remote(keeps.at[o], keeps.at[o], keep_s.at[o], keep_r.at[o], at(pos, col)).wait_recv()
        remote(cut.at[o], got.at[o], cut_s.at[o], cut_r.at[o], at(pos, col)).wait_recv()
    run = [jnp.zeros((sr, MEM), F32) for _ in range(4)]
    decayed = [jnp.ones((1, MEM), F32) for _ in range(2)]
    decayed_at = []
    for b in range(NY):
        decayed_at.append(list(decayed))
        for h in range(2):
            kb = keeps[b, h : h + 1, :]
            for hl in (2 * h, 2 * h + 1):
                inner[b, hl] = run[hl]
                run[hl] = run[hl] * kb + got[b, hl].astype(F32)
            decayed[h] = decayed[h] * kb

    def tiles():
        t = 0
        for hl in range(4):
            for dh in range(dh_n):
                for jh in range(2):
                    yield t // tps, t % tps, hl, slice(dh * SUB, (dh + 1) * SUB), slice(jh * LANES, (jh + 1) * LANES)
                    t += 1

    for owner, slot, hl, ds_, js in tiles():
        tot[owner, slot, 0] = run[hl][ds_, js]
        tot[owner, slot, 1] = jnp.broadcast_to(decayed[hl // 2][:, js], (SUB, LANES))
    rows_in[r] = tot[r]

    def tot_copy(i):
        to = in_rows(i)
        return remote(tot.at[to], rows_in.at[r], tot_s.at[to], tot_r.at[r], at(to * NY + y, col))

    for i in range(1, nr):
        tot_copy(i).start()

    def halo_got(k):
        remote(halo.at[k - 1], halo.at[k], halo_s.at[k - 1], halo_r.at[k], at(pos, col)).wait_recv()

    halo_copy(0).start()
    pump(1)

    for i in range(1, nr):
        o = in_rows(i)
        remote(tot.at[o], rows_in.at[o], tot_s.at[o], tot_r.at[o], at(pos, col)).wait_recv()
    for slot in range(tps):
        e = jnp.zeros((SUB, LANES), F32)
        for rr in range(nr):
            ent[rr, slot] = e
            e = e * rows_in[rr, slot, 1] + rows_in[rr, slot, 0]
    ent_in[r] = ent[r]

    def ent_copy(i):
        to = in_rows(i)
        return remote(ent.at[to], ent_in.at[r], ent_s.at[to], ent_r.at[r], at(to * NY + y, col))

    for i in range(1, nr):
        ent_copy(i).start()

    halo_got(1)
    halo_copy(1).start()
    pump(2)

    for i in range(1, nr):
        o = in_rows(i)
        remote(ent.at[o], ent_in.at[o], ent_s.at[o], ent_r.at[o], at(pos, col)).wait_recv()
    for owner, slot, hl, ds_, js in tiles():
        e = ent_in[owner, slot]
        for b in range(NY):
            whole = inner[b, hl, ds_, js] + e * decayed_at[b][hl // 2][:, js]
            inner[b, hl, ds_, js] = whole
    for b in range(NY):
        for hl in range(4):
            back[b, hl] = inner[b, hl].astype(BF16)
    back_in[y] = back[y]

    def back_copy(i):
        to = in_row(i)
        return remote(back.at[to], back_in.at[y], back_s.at[to], back_r.at[y], at(r * NY + to, col))

    for i in range(1, NY):
        back_copy(i).start()

    halo_got(2)
    halo_copy(2).start()
    pump(3)

    for i in range(1, NY):
        o = in_row(i)
        remote(back.at[o], back_in.at[o], back_s.at[o], back_r.at[o], at(pos, col)).wait_recv()
    read = []
    for h in range(2):
        kh = keep2[h : h + 1, :]
        state = []
        for layer in range(2):
            hl = 2 * h + layer
            entering = jnp.concatenate([back_in[s, hl] for s in range(NY)], 0).astype(F32)
            state.append(entering * kh + upd[hl])
        fast_first = (m1_ref[h].astype(F32) + state[0]).astype(BF16)
        fast_second = (m2_ref[h].astype(F32).T + state[1]).astype(BF16)
        zq = dot(q_ref[:, h * HD : (h + 1) * HD], fast_first, 1, 0)
        recall = (zq * jax.nn.sigmoid(zq)).astype(BF16)
        read.append(dot(recall, fast_second, 1, 1).astype(BF16))
    reads[zh] = jnp.concatenate(read, 1)

    def read_copy(g):
        return remote(
            reads.at[zh], reads.at[zh], read_s.at[g], read_r.at[zh], at(pos, lax.rem(col + 2 * g, n_col))
        )

    for g in range(1, groups):
        read_copy(g).start()

    halo_got(3)
    halo_copy(3).start()
    halo_got(4)
    scale = 1.0 / math.sqrt(HD)
    causal = lax.broadcasted_iota(jnp.int32, (HD, HD), 1) <= lax.broadcasted_iota(jnp.int32, (HD, HD), 0)
    clear = jnp.ones((1, HD), F32)
    clear_at = []
    for k in range(1, WMAX + 1):
        clear = clear * (1.0 - halo[k - 1, 2 * HD : 2 * HD + 16, 0:HD].astype(F32)[0:1])
        clear_at.append(clear * jnp.where(pos >= k, 1.0, 0.0))
    for h in range(2):
        cols = slice(h * HD, (h + 1) * HD)
        qh = q_ref[:, cols]
        s = [jnp.where(causal, dot(qh, halo[0, 0:HD, cols], 1, 1) * scale, -1e30)]
        for k in range(1, WMAX + 1):
            ok = clear_at[k - 1] * jnp.where(win_ref[h] >= k, 1.0, 0.0)
            s.append(jnp.where(ok > 0.5, dot(qh, halo[k, 0:HD, cols], 1, 1) * scale, -1e30))
        s = jnp.concatenate(s, 1)
        top = jnp.max(s, axis=1, keepdims=True)
        e = jnp.exp(s - top)
        w = (e / jnp.sum(e, axis=1, keepdims=True)).astype(BF16)
        vals = jnp.concatenate([halo[k, HD : 2 * HD, cols] for k in range(WMAX + 1)], 0)
        att_ref[:, cols] = dot(w, vals, 1, 0).astype(BF16)

    pump_last()
    for g in range(1, groups):
        o = lax.rem(zh + g, groups)
        remote(reads.at[o], reads.at[o], read_s.at[g], read_r.at[o], at(pos, col)).wait_recv()
    left = jnp.concatenate([reads[g] for g in range(groups)], 1)

    def part_copy(c):
        return remote(part.at[c], part_in.at[c], part_s.at[c], part_r.at[c], at(pos, sibling))

    for c in range(n_out):
        cs = slice(c * OUT_COLS, (c + 1) * OUT_COLS)
        right = jnp.concatenate([wall[g, :, cs] for g in range(groups)], 0)
        part[c] = dot(left, right, 1, 0).astype(BF16)
        part_copy(c).start()
    for c in range(n_out):
        cs = slice(c * OUT_COLS, (c + 1) * OUT_COLS)
        part_copy(c).wait_recv()
        out_ref[:, cs] = (part[c].astype(F32) + part_in[c].astype(F32)).astype(BF16)

    for i in range(1, NY):
        keep_copy(i).wait_send()
        cut_copy(i).wait_send()
        back_copy(i).wait_send()
    for i in range(1, nr):
        tot_copy(i).wait_send()
        ent_copy(i).wait_send()
    for k in range(WMAX):
        halo_copy(k).wait_send()
    for g in range(1, groups):
        read_copy(g).wait_send()
    for way in range(2):
        for c in range(PARTS):
            wall_copy(way, send_g[way], c).wait_send()
        for i in range(1, nx):
            across_copy(way, i).wait_send()
    for c in range(n_out):
        part_copy(c).wait_send()


def solution(mesh):
    n_stretch, n_col = mesh.shape["stretch"], mesh.shape["col"]
    nr, groups, sr = n_stretch // NY, n_col // 2, HD // NY
    tps = 4 * (sr // SUB) * 2 // nr

    def shards(queries, keys, values, memory_first, memory_second_weight, out_weight, decay, boundary, win_blocks):
        d = out_weight.shape[1]
        hbm = pl.BlockSpec(memory_space=pltpu.HBM)
        vmem = pl.BlockSpec(memory_space=pltpu.VMEM)
        dma = pltpu.SemaphoreType.DMA
        return tuple(
            pl.pallas_call(
                functools.partial(kernel, n_stretch, n_col),
                out_shape=(
                    jax.ShapeDtypeStruct((HD, 2 * HD), BF16),
                    jax.ShapeDtypeStruct((HD, d), BF16),
                ),
                in_specs=[hbm] * 8 + [pl.BlockSpec(memory_space=pltpu.SMEM)],
                out_specs=(vmem, vmem),
                scratch_shapes=[
                    pltpu.VMEM((HD, 2 * HD), BF16),
                    pltpu.VMEM((2, HD, MEM), BF16),
                    pltpu.VMEM((2, MEM, HD), BF16),
                    pltpu.VMEM((1, 2, MEM), F32),
                    pltpu.SMEM((2,), jnp.int32),
                    pltpu.VMEM((WMAX + 1, 2 * HD + 16, 2 * HD), BF16),
                    pltpu.VMEM((NY, SUB, MEM), F32),
                    pltpu.VMEM((4, HD, MEM), F32),
                    pltpu.VMEM((NY, 4, sr, MEM), BF16),
                    pltpu.VMEM((NY, 4, sr, MEM), BF16),
                    pltpu.VMEM((NY, 4, sr, MEM), F32),
                    pltpu.VMEM((nr, tps, 2, SUB, LANES), F32),
                    pltpu.VMEM((nr, tps, 2, SUB, LANES), F32),
                    pltpu.VMEM((nr, tps, SUB, LANES), F32),
                    pltpu.VMEM((nr, tps, SUB, LANES), F32),
                    pltpu.VMEM((NY, 4, sr, MEM), BF16),
                    pltpu.VMEM((NY, 4, sr, MEM), BF16),
                    pltpu.VMEM((groups, 2 * HD, d), BF16),
                    pltpu.VMEM((groups, HD, 2 * HD), BF16),
                    pltpu.VMEM((d // OUT_COLS, HD, OUT_COLS), BF16),
                    pltpu.VMEM((d // OUT_COLS, HD, OUT_COLS), BF16),
                    dma((7,)),
                    dma((WMAX + 1,)),
                    dma((WMAX + 1,)),
                    dma((NY,)),
                    dma((NY,)),
                    dma((NY,)),
                    dma((NY,)),
                    dma((nr,)),
                    dma((nr,)),
                    dma((nr,)),
                    dma((nr,)),
                    dma((NY,)),
                    dma((NY,)),
                    dma((PARTS,)),
                    dma((PARTS,)),
                    dma((PARTS,)),
                    dma((PARTS,)),
                    dma((2, nr // NZ)),
                    dma((2, nr // NZ)),
                    dma,
                    dma((groups,)),
                    dma((groups,)),
                    dma((d // OUT_COLS,)),
                    dma((d // OUT_COLS,)),
                ],
                compiler_params=pltpu.CompilerParams(
                    collective_id=0, has_side_effects=True, vmem_limit_bytes=48 * 2**20
                ),
            )(
                *(
                    pltpu.with_memory_space_constraint(x, pltpu.HBM)
                    for x in (
                        queries,
                        keys,
                        values,
                        memory_first,
                        memory_second_weight,
                        out_weight,
                        decay,
                        win_blocks,
                    )
                ),
                boundary,
            )
        )

    placed = (
        P("stretch", "col"),
        P("stretch", "col"),
        P("stretch", "col"),
        P("col", None, None),
        P("col", None, None),
        P("col", None),
        P("stretch", "col", None),
        P("stretch"),
        P("col"),
    )
    return jax.shard_map(
        shards,
        mesh=mesh,
        in_specs=placed,
        out_specs=(P("stretch", "col"), P("stretch", None)),
        check_vma=False,
    )
```

```python
import functools
import math

import jax
import jax.numpy as jnp
from jax import lax
from jax.experimental import pallas as pl
from jax.experimental.pallas import tpu as pltpu
from jax.sharding import PartitionSpec as P

HD = 128
MEM = 256
WMAX = 4
NY = 8
NZ = 4
PARTS = 2
DUE = (((0, 1), (), ()), ((0,), (1,), ()), ((), (0,), (1,)), ((), (), (0, 1)))
LANES = 128
SUB = 8
OUT_COLS = 512
MESH = pl.DeviceIdType.MESH
BF16 = jnp.bfloat16
F32 = jnp.float32


def dot(a, b, ca, cb):
    return lax.dot_general(a, b, (((ca,), (cb,)), ((), ())), preferred_element_type=F32)


def kernel(
    n_stretch,
    n_col,
    q_hbm,
    k_hbm,
    v_hbm,
    m1_hbm,
    m2_hbm,
    wo_ref,
    decay_hbm,
    win_hbm,
    bnd_ref,
    att_ref,
    out_ref,
    q_ref,
    m1_ref,
    m2_ref,
    decay_ref,
    win_ref,
    halo,
    keeps,
    upd,
    cut,
    got,
    inner,
    tot,
    rows_in,
    ent,
    ent_in,
    back,
    back_in,
    wall,
    reads,
    part,
    part_in,
    in_s,
    halo_s,
    halo_r,
    keep_s,
    keep_r,
    cut_s,
    cut_r,
    tot_s,
    tot_r,
    ent_s,
    ent_r,
    back_s,
    back_r,
    up_s,
    up_r,
    down_s,
    down_r,
    across_s,
    across_r,
    wall_l,
    read_s,
    read_r,
    part_s,
    part_r,
):
    nr = n_stretch // NY
    nx = nr // NZ
    groups = n_col // 2
    sr = HD // NY
    dh_n = sr // SUB
    tps = 4 * dh_n * 2 // nr
    n_out = out_ref.shape[1] // OUT_COLS

    pos = lax.axis_index("stretch")
    col = lax.axis_index("col")
    y = lax.rem(pos, NY)
    r = pos // NY
    zl = lax.rem(r, NZ)
    xs = r // NZ
    zh = col // 2
    core = lax.rem(col, 2)
    sibling = col + 1 - 2 * core

    def at(s, c):
        return {"stretch": s, "col": c}

    def in_row(i):
        return lax.rem(y + i, NY)

    def in_rows(i):
        return lax.rem(r + i, nr)

    ends, starts = zl == NZ - 1, zl == 0
    above = at(
        jnp.where(ends, pos - (NZ - 1) * NY, pos + NY), jnp.where(ends, lax.rem(col + 2, n_col), col)
    )
    below = at(
        jnp.where(starts, pos + (NZ - 1) * NY, pos - NY), jnp.where(starts, lax.rem(col + n_col - 2, n_col), col)
    )

    def remote(src, dst, send, recv, where):
        return pltpu.make_async_remote_copy(
            src_ref=src, dst_ref=dst, send_sem=send, recv_sem=recv, device_id=where, device_id_type=MESH
        )

    barrier = pltpu.get_barrier_semaphore()

    def greet(where):
        pl.semaphore_signal(barrier, inc=1, device_id=where, device_id_type=MESH)

    for i in range(1, NY):
        greet(at(r * NY + in_row(i), col))
    for i in range(1, nr):
        greet(at(in_rows(i) * NY + y, col))
    for i in (1, 2, n_stretch - 1, n_stretch - 2):
        greet(at(lax.rem(pos + i, n_stretch), col))
    for g in range(1, groups):
        greet(at(pos, lax.rem(col + 2 * g, n_col)))
    greet(at(pos, sibling))
    greet(above)
    greet(below)
    greeted = (NY - 1) + (nr - 1) + 4 + (groups - 1) + 1 + 2

    own = halo.at[0]
    loads = [
        pltpu.make_async_copy(src, dst, in_s.at[i])
        for i, (src, dst) in enumerate(
            (
                (k_hbm, own.at[0:HD]),
                (m1_hbm, m1_ref),
                (m2_hbm, m2_ref),
                (v_hbm, own.at[HD : 2 * HD]),
                (decay_hbm, decay_ref),
                (q_hbm, q_ref),
                (win_hbm, win_ref),
            )
        )
    ]
    for load in loads:
        load.start()
    own_w = pltpu.make_async_copy(wo_ref, wall.at[zh], wall_l)
    own_w.start()
    for load in loads:
        load.wait()
    flag = bnd_ref[0].astype(F32)
    halo[0, 2 * HD :, :] = jnp.full((16, 2 * HD), flag, F32).astype(BF16)
    keep2 = decay_ref[0] * (1.0 - flag)
    keeps[y] = jnp.concatenate([keep2, jnp.zeros((SUB - 2, MEM), F32)], 0)

    eta = 1.0 / (HD * math.sqrt(n_stretch))
    for h in range(2):
        cols = slice(h * HD, (h + 1) * HD)
        kh = halo[0, 0:HD, cols]
        m2 = m2_ref[h]
        z = dot(kh, m1_ref[h], 1, 0)
        sig = jax.nn.sigmoid(z)
        hidden = (z * sig).astype(BF16)
        err = (dot(hidden, m2, 1, 0) - halo[0, HD : 2 * HD, cols].astype(F32)).astype(BF16)
        dz = (dot(err, m2, 1, 1) * (sig * (1.0 + z * (1.0 - sig)))).astype(BF16)
        for layer, grad in enumerate((dot(kh, dz, 0, 0), dot(err, hidden, 0, 0))):
            u = -eta * grad
            upd[2 * h + layer] = u
            for s in range(NY):
                cut[s, 2 * h + layer] = u[s * sr : (s + 1) * sr].astype(BF16)
    got[y] = cut[y]

    pl.semaphore_wait(barrier, greeted)

    def keep_copy(i):
        to = in_row(i)
        return remote(keeps.at[y], keeps.at[y], keep_s.at[to], keep_r.at[y], at(r * NY + to, col))

    def cut_copy(i):
        to = in_row(i)
        return remote(cut.at[to], got.at[y], cut_s.at[to], cut_r.at[y], at(r * NY + to, col))

    def halo_copy(k, ahead):
        to = lax.rem(pos + ahead, n_stretch)
        return remote(halo.at[k], halo.at[k + ahead], halo_s.at[k + ahead - 1], halo_r.at[k + ahead], at(to, col))

    rows_c = 2 * HD // nx // PARTS
    wait_g = lax.rem(zh + groups - 1, groups), lax.rem(zh + 1, groups)
    send_g = jnp.where(ends, zh, wait_g[0]), jnp.where(starts, zh, wait_g[1])
    chain = zl, NZ - 1 - zl

    def share(g, xx, c):
        return wall.at[g, pl.ds(pl.multiple_of((xx * PARTS + c) * rows_c, rows_c), rows_c)]

    def wall_copy(way, g, c):
        piece = share(g, xs, c)
        sem_s, sem_r = ((up_s, up_r), (down_s, down_r))[way]
        return remote(piece, piece, sem_s.at[c], sem_r.at[c], (above, below)[way])

    def across_copy(way, c, i):
        piece = share(wait_g[way], xs, c)
        to = lax.rem(pos + i * NY * NZ, n_stretch)
        return remote(piece, piece, across_s.at[way, c, i], across_r.at[way, c, i], at(to, col))

    def across_got(way, c, i):
        piece = share(wait_g[way], lax.rem(xs + nx - i, nx), c)
        remote(piece, piece, across_s.at[way, c, i], across_r.at[way, c, i], at(pos, col)).wait_recv()

    def pump(point):
        for way in range(2):
            for d in range(NZ):

                @pl.when(chain[way] == d)
                def _():
                    for c in DUE[d][point]:
                        wall_copy(way, wait_g[way], c).wait_recv()
                        if d < NZ - 1:
                            wall_copy(way, send_g[way], c).start()
                        for i in range(1, nx):
                            across_copy(way, c, i).start()

    def pump_first():
        for way in range(2):

            @pl.when(chain[way] == NZ - 1)
            def _():
                for c in range(PARTS):
                    wall_copy(way, zh, c).start()

    def pump_last():
        for way in range(2):
            for c in range(PARTS):
                for i in range(1, nx):
                    across_got(way, c, i)

    for i in range(1, NY):
        keep_copy(i).start()
    for i in range(1, NY):
        cut_copy(i).start()
    own_w.wait()
    pump_first()

    for i in range(1, NY):
        o = in_row(i)
        remote(keeps.at[o], keeps.at[o], keep_s.at[o], keep_r.at[o], at(pos, col)).wait_recv()
        remote(cut.at[o], got.at[o], cut_s.at[o], cut_r.at[o], at(pos, col)).wait_recv()
    run = [jnp.zeros((sr, MEM), F32) for _ in range(4)]
    decayed = [jnp.ones((1, MEM), F32) for _ in range(2)]
    decayed_at = []
    for b in range(NY):
        decayed_at.append(list(decayed))
        for h in range(2):
            kb = keeps[b, h : h + 1, :]
            for hl in (2 * h, 2 * h + 1):
                inner[b, hl] = run[hl]
                run[hl] = run[hl] * kb + got[b, hl].astype(F32)
            decayed[h] = decayed[h] * kb

    def tiles():
        t = 0
        for hl in range(4):
            for dh in range(dh_n):
                for jh in range(2):
                    yield t // tps, t % tps, hl, slice(dh * SUB, (dh + 1) * SUB), slice(jh * LANES, (jh + 1) * LANES)
                    t += 1

    for owner, slot, hl, ds_, js in tiles():
        tot[owner, slot, 0] = run[hl][ds_, js]
        tot[owner, slot, 1] = jnp.broadcast_to(decayed[hl // 2][:, js], (SUB, LANES))
    rows_in[r] = tot[r]

    def tot_copy(i):
        to = in_rows(i)
        return remote(tot.at[to], rows_in.at[r], tot_s.at[to], tot_r.at[r], at(to * NY + y, col))

    for i in range(1, nr):
        tot_copy(i).start()

    def halo_got(k):
        remote(halo.at[0], halo.at[k], halo_s.at[k - 1], halo_r.at[k], at(pos, col)).wait_recv()

    halo_copy(0, 2).start()
    halo_copy(0, 1).start()
    pump(0)

    for i in range(1, nr):
        o = in_rows(i)
        remote(tot.at[o], rows_in.at[o], tot_s.at[o], tot_r.at[o], at(pos, col)).wait_recv()
    for slot in range(tps):
        e = jnp.zeros((SUB, LANES), F32)
        for rr in range(nr):
            ent[rr, slot] = e
            e = e * rows_in[rr, slot, 1] + rows_in[rr, slot, 0]
    ent_in[r] = ent[r]

    def ent_copy(i):
        to = in_rows(i)
        return remote(ent.at[to], ent_in.at[r], ent_s.at[to], ent_r.at[r], at(to * NY + y, col))

    for i in range(1, nr):
        ent_copy(i).start()

    pump(1)

    for i in range(1, nr):
        o = in_rows(i)
        remote(ent.at[o], ent_in.at[o], ent_s.at[o], ent_r.at[o], at(pos, col)).wait_recv()
    for owner, slot, hl, ds_, js in tiles():
        e = ent_in[owner, slot]
        for b in range(NY):
            whole = inner[b, hl, ds_, js] + e * decayed_at[b][hl // 2][:, js]
            inner[b, hl, ds_, js] = whole
    for b in range(NY):
        for hl in range(4):
            back[b, hl] = inner[b, hl].astype(BF16)
    back_in[y] = back[y]

    def back_copy(i):
        to = in_row(i)
        return remote(back.at[to], back_in.at[y], back_s.at[to], back_r.at[y], at(r * NY + to, col))

    for i in range(1, NY):
        back_copy(i).start()

    pump(2)

    for i in range(1, NY):
        o = in_row(i)
        remote(back.at[o], back_in.at[o], back_s.at[o], back_r.at[o], at(pos, col)).wait_recv()
    read = []
    for h in range(2):
        kh = keep2[h : h + 1, :]
        state = []
        for layer in range(2):
            hl = 2 * h + layer
            entering = jnp.concatenate([back_in[s, hl] for s in range(NY)], 0).astype(F32)
            state.append(entering * kh + upd[hl])
        fast_first = (m1_ref[h].astype(F32) + state[0]).astype(BF16)
        fast_second = (m2_ref[h].astype(F32).T + state[1]).astype(BF16)
        zq = dot(q_ref[:, h * HD : (h + 1) * HD], fast_first, 1, 0)
        recall = (zq * jax.nn.sigmoid(zq)).astype(BF16)
        read.append(dot(recall, fast_second, 1, 1).astype(BF16))
    reads[zh] = jnp.concatenate(read, 1)

    def read_copy(g):
        return remote(
            reads.at[zh], reads.at[zh], read_s.at[g], read_r.at[zh], at(pos, lax.rem(col + 2 * g, n_col))
        )

    for g in range(1, groups):
        read_copy(g).start()

    halo_got(2)
    halo_copy(2, 2).start()
    halo_copy(2, 1).start()
    pump_last()
    for g in range(1, groups):
        o = lax.rem(zh + g, groups)
        remote(reads.at[o], reads.at[o], read_s.at[g], read_r.at[o], at(pos, col)).wait_recv()
    left = jnp.concatenate([reads[g] for g in range(groups)], 1)

    def part_copy(c):
        return remote(part.at[c], part_in.at[c], part_s.at[c], part_r.at[c], at(pos, sibling))

    for c in range(n_out):
        cs = slice(c * OUT_COLS, (c + 1) * OUT_COLS)
        right = jnp.concatenate([wall[g, :, cs] for g in range(groups)], 0)
        part[c] = dot(left, right, 1, 0).astype(BF16)
        part_copy(c).start()
    halo_got(1)
    halo_got(3)
    halo_got(4)
    scale = 1.0 / math.sqrt(HD)
    causal = lax.broadcasted_iota(jnp.int32, (HD, HD), 1) <= lax.broadcasted_iota(jnp.int32, (HD, HD), 0)
    clear = jnp.ones((1, HD), F32)
    clear_at = []
    for k in range(1, WMAX + 1):
        clear = clear * (1.0 - halo[k - 1, 2 * HD : 2 * HD + 16, 0:HD].astype(F32)[0:1])
        clear_at.append(clear * jnp.where(pos >= k, 1.0, 0.0))
    for h in range(2):
        cols = slice(h * HD, (h + 1) * HD)
        qh = q_ref[:, cols]
        s = [jnp.where(causal, dot(qh, halo[0, 0:HD, cols], 1, 1) * scale, -1e30)]
        for k in range(1, WMAX + 1):
            ok = clear_at[k - 1] * jnp.where(win_ref[h] >= k, 1.0, 0.0)
            s.append(jnp.where(ok > 0.5, dot(qh, halo[k, 0:HD, cols], 1, 1) * scale, -1e30))
        s = jnp.concatenate(s, 1)
        top = jnp.max(s, axis=1, keepdims=True)
        e = jnp.exp(s - top)
        w = (e / jnp.sum(e, axis=1, keepdims=True)).astype(BF16)
        vals = jnp.concatenate([halo[k, HD : 2 * HD, cols] for k in range(WMAX + 1)], 0)
        att_ref[:, cols] = dot(w, vals, 1, 0).astype(BF16)

    for c in range(n_out):
        cs = slice(c * OUT_COLS, (c + 1) * OUT_COLS)
        part_copy(c).wait_recv()
        out_ref[:, cs] = (part[c].astype(F32) + part_in[c].astype(F32)).astype(BF16)

    for i in range(1, NY):
        keep_copy(i).wait_send()
        cut_copy(i).wait_send()
        back_copy(i).wait_send()
    for i in range(1, nr):
        tot_copy(i).wait_send()
        ent_copy(i).wait_send()
    for k in (0, 2):
        for ahead in (1, 2):
            halo_copy(k, ahead).wait_send()
    for g in range(1, groups):
        read_copy(g).wait_send()
    for way in range(2):
        for c in range(PARTS):
            wall_copy(way, send_g[way], c).wait_send()
            for i in range(1, nx):
                across_copy(way, c, i).wait_send()
    for c in range(n_out):
        part_copy(c).wait_send()


def solution(mesh):
    n_stretch, n_col = mesh.shape["stretch"], mesh.shape["col"]
    nr, groups, sr = n_stretch // NY, n_col // 2, HD // NY
    tps = 4 * (sr // SUB) * 2 // nr

    def shards(queries, keys, values, memory_first, memory_second_weight, out_weight, decay, boundary, win_blocks):
        d = out_weight.shape[1]
        hbm = pl.BlockSpec(memory_space=pltpu.HBM)
        vmem = pl.BlockSpec(memory_space=pltpu.VMEM)
        dma = pltpu.SemaphoreType.DMA
        return tuple(
            pl.pallas_call(
                functools.partial(kernel, n_stretch, n_col),
                out_shape=(
                    jax.ShapeDtypeStruct((HD, 2 * HD), BF16),
                    jax.ShapeDtypeStruct((HD, d), BF16),
                ),
                in_specs=[hbm] * 8 + [pl.BlockSpec(memory_space=pltpu.SMEM)],
                out_specs=(vmem, vmem),
                scratch_shapes=[
                    pltpu.VMEM((HD, 2 * HD), BF16),
                    pltpu.VMEM((2, HD, MEM), BF16),
                    pltpu.VMEM((2, MEM, HD), BF16),
                    pltpu.VMEM((1, 2, MEM), F32),
                    pltpu.SMEM((2,), jnp.int32),
                    pltpu.VMEM((WMAX + 1, 2 * HD + 16, 2 * HD), BF16),
                    pltpu.VMEM((NY, SUB, MEM), F32),
                    pltpu.VMEM((4, HD, MEM), F32),
                    pltpu.VMEM((NY, 4, sr, MEM), BF16),
                    pltpu.VMEM((NY, 4, sr, MEM), BF16),
                    pltpu.VMEM((NY, 4, sr, MEM), F32),
                    pltpu.VMEM((nr, tps, 2, SUB, LANES), F32),
                    pltpu.VMEM((nr, tps, 2, SUB, LANES), F32),
                    pltpu.VMEM((nr, tps, SUB, LANES), F32),
                    pltpu.VMEM((nr, tps, SUB, LANES), F32),
                    pltpu.VMEM((NY, 4, sr, MEM), BF16),
                    pltpu.VMEM((NY, 4, sr, MEM), BF16),
                    pltpu.VMEM((groups, 2 * HD, d), BF16),
                    pltpu.VMEM((groups, HD, 2 * HD), BF16),
                    pltpu.VMEM((d // OUT_COLS, HD, OUT_COLS), BF16),
                    pltpu.VMEM((d // OUT_COLS, HD, OUT_COLS), BF16),
                    dma((7,)),
                    dma((WMAX + 1,)),
                    dma((WMAX + 1,)),
                    dma((NY,)),
                    dma((NY,)),
                    dma((NY,)),
                    dma((NY,)),
                    dma((nr,)),
                    dma((nr,)),
                    dma((nr,)),
                    dma((nr,)),
                    dma((NY,)),
                    dma((NY,)),
                    dma((PARTS,)),
                    dma((PARTS,)),
                    dma((PARTS,)),
                    dma((PARTS,)),
                    dma((2, PARTS, nr // NZ)),
                    dma((2, PARTS, nr // NZ)),
                    dma,
                    dma((groups,)),
                    dma((groups,)),
                    dma((d // OUT_COLS,)),
                    dma((d // OUT_COLS,)),
                ],
                compiler_params=pltpu.CompilerParams(
                    collective_id=0, has_side_effects=True, vmem_limit_bytes=48 * 2**20
                ),
            )(
                *(
                    pltpu.with_memory_space_constraint(x, pltpu.HBM)
                    for x in (
                        queries,
                        keys,
                        values,
                        memory_first,
                        memory_second_weight,
                        out_weight,
                        decay,
                        win_blocks,
                    )
                ),
                boundary,
            )
        )

    placed = (
        P("stretch", "col"),
        P("stretch", "col"),
        P("stretch", "col"),
        P("col", None, None),
        P("col", None, None),
        P("col", None),
        P("stretch", "col", None),
        P("stretch"),
        P("col"),
    )
    return jax.shard_map(
        shards,
        mesh=mesh,
        in_specs=placed,
        out_specs=(P("stretch", "col"), P("stretch", None)),
        check_vma=False,
    )
```

```python
import functools
import math

import jax
import jax.numpy as jnp
from jax import lax
from jax.experimental import pallas as pl
from jax.experimental.pallas import tpu as pltpu
from jax.sharding import PartitionSpec as P

HD = 128
MEM = 256
WMAX = 4
NY = 8
NZ = 4
PARTS = 2
DUE = (((0, 1), (), ()), ((0,), (1,), ()), ((), (0,), (1,)), ((), (), (0, 1)))
LANES = 128
SUB = 8
OUT_COLS = 512
MESH = pl.DeviceIdType.MESH
BF16 = jnp.bfloat16
F32 = jnp.float32


def dot(a, b, ca, cb):
    return lax.dot_general(a, b, (((ca,), (cb,)), ((), ())), preferred_element_type=F32)


def kernel(
    n_stretch,
    n_col,
    q_hbm,
    k_hbm,
    v_hbm,
    m1_hbm,
    m2_hbm,
    wo_ref,
    decay_hbm,
    win_hbm,
    bnd_ref,
    att_ref,
    out_ref,
    q_ref,
    m1_ref,
    m2_ref,
    decay_ref,
    win_ref,
    halo,
    keeps,
    upd,
    cut,
    got,
    inner,
    tot,
    rows_in,
    ent,
    ent_in,
    back,
    back_in,
    wall,
    reads,
    part,
    part_in,
    in_s,
    halo_s,
    halo_r,
    keep_s,
    keep_r,
    cut_s,
    cut_r,
    tot_s,
    tot_r,
    ent_s,
    ent_r,
    back_s,
    back_r,
    up_s,
    up_r,
    down_s,
    down_r,
    across_s,
    across_r,
    wall_l,
    read_s,
    read_r,
    part_s,
    part_r,
):
    nr = n_stretch // NY
    nx = nr // NZ
    groups = n_col // 2
    sr = HD // NY
    dh_n = sr // SUB
    tps = 4 * dh_n * 2 // nr
    n_out = out_ref.shape[1] // OUT_COLS

    pos = lax.axis_index("stretch")
    col = lax.axis_index("col")
    y = lax.rem(pos, NY)
    r = pos // NY
    zl = lax.rem(r, NZ)
    xs = r // NZ
    zh = col // 2
    core = lax.rem(col, 2)
    sibling = col + 1 - 2 * core

    def at(s, c):
        return {"stretch": s, "col": c}

    def in_row(i):
        return lax.rem(y + i, NY)

    def in_rows(i):
        return lax.rem(r + i, nr)

    ends, starts = zl == NZ - 1, zl == 0
    above = at(
        jnp.where(ends, pos - (NZ - 1) * NY, pos + NY), jnp.where(ends, lax.rem(col + 2, n_col), col)
    )
    below = at(
        jnp.where(starts, pos + (NZ - 1) * NY, pos - NY), jnp.where(starts, lax.rem(col + n_col - 2, n_col), col)
    )

    def remote(src, dst, send, recv, where):
        return pltpu.make_async_remote_copy(
            src_ref=src, dst_ref=dst, send_sem=send, recv_sem=recv, device_id=where, device_id_type=MESH
        )

    barrier = pltpu.get_barrier_semaphore()

    def greet(where):
        pl.semaphore_signal(barrier, inc=1, device_id=where, device_id_type=MESH)

    for i in range(1, NY):
        greet(at(r * NY + in_row(i), col))
    for i in range(1, nr):
        greet(at(in_rows(i) * NY + y, col))
    for i in (1, 2, n_stretch - 1, n_stretch - 2):
        greet(at(lax.rem(pos + i, n_stretch), col))
    for g in range(1, groups):
        greet(at(pos, lax.rem(col + 2 * g, n_col)))
    greet(at(pos, sibling))
    greet(above)
    greet(below)
    greeted = (NY - 1) + (nr - 1) + 4 + (groups - 1) + 1 + 2

    own = halo.at[0]
    loads = [
        pltpu.make_async_copy(src, dst, in_s.at[i])
        for i, (src, dst) in enumerate(
            (
                (k_hbm, own.at[0:HD]),
                (m1_hbm, m1_ref),
                (m2_hbm, m2_ref),
                (v_hbm, own.at[HD : 2 * HD]),
                (decay_hbm, decay_ref),
                (q_hbm, q_ref),
                (win_hbm, win_ref),
            )
        )
    ]
    for load in loads:
        load.start()
    own_w = pltpu.make_async_copy(wo_ref, wall.at[zh], wall_l)
    own_w.start()
    for load in loads:
        load.wait()
    flag = bnd_ref[0].astype(F32)
    halo[0, 2 * HD :, :] = jnp.full((16, 2 * HD), flag, F32).astype(BF16)
    keep2 = decay_ref[0] * (1.0 - flag)
    keeps[y] = jnp.concatenate([keep2, jnp.zeros((SUB - 2, MEM), F32)], 0)

    eta = 1.0 / (HD * math.sqrt(n_stretch))
    for h in range(2):
        cols = slice(h * HD, (h + 1) * HD)
        kh = halo[0, 0:HD, cols]
        m2 = m2_ref[h]
        z = dot(kh, m1_ref[h], 1, 0)
        sig = jax.nn.sigmoid(z)
        hidden = (z * sig).astype(BF16)
        err = (dot(hidden, m2, 1, 0) - halo[0, HD : 2 * HD, cols].astype(F32)).astype(BF16)
        dz = (dot(err, m2, 1, 1) * (sig * (1.0 + z * (1.0 - sig)))).astype(BF16)
        for layer, grad in enumerate((dot(kh, dz, 0, 0), dot(err, hidden, 0, 0))):
            u = -eta * grad
            upd[2 * h + layer] = u
            for s in range(NY):
                cut[s, 2 * h + layer] = u[s * sr : (s + 1) * sr].astype(BF16)
    got[y] = cut[y]

    pl.semaphore_wait(barrier, greeted)

    def keep_copy(i):
        to = in_row(i)
        return remote(keeps.at[y], keeps.at[y], keep_s.at[to], keep_r.at[y], at(r * NY + to, col))

    def cut_copy(i):
        to = in_row(i)
        return remote(cut.at[to], got.at[y], cut_s.at[to], cut_r.at[y], at(r * NY + to, col))

    def halo_copy(k, ahead):
        to = lax.rem(pos + ahead, n_stretch)
        return remote(halo.at[k], halo.at[k + ahead], halo_s.at[k + ahead - 1], halo_r.at[k + ahead], at(to, col))

    rows_c = 2 * HD // nx // PARTS
    wait_g = lax.rem(zh + groups - 1, groups), lax.rem(zh + 1, groups)
    send_g = jnp.where(ends, zh, wait_g[0]), jnp.where(starts, zh, wait_g[1])
    chain = zl, NZ - 1 - zl

    def share(g, xx, c):
        return wall.at[g, pl.ds(pl.multiple_of((xx * PARTS + c) * rows_c, rows_c), rows_c)]

    def wall_copy(way, g, c):
        piece = share(g, xs, c)
        sem_s, sem_r = ((up_s, up_r), (down_s, down_r))[way]
        return remote(piece, piece, sem_s.at[c], sem_r.at[c], (above, below)[way])

    def across_copy(way, c, i):
        piece = share(wait_g[way], xs, c)
        to = lax.rem(pos + i * NY * NZ, n_stretch)
        return remote(piece, piece, across_s.at[way, c, i], across_r.at[way, c, i], at(to, col))

    def across_got(way, c, i):
        piece = share(wait_g[way], lax.rem(xs + nx - i, nx), c)
        remote(piece, piece, across_s.at[way, c, i], across_r.at[way, c, i], at(pos, col)).wait_recv()

    def pump(point):
        for way in range(2):
            for d in range(NZ):

                @pl.when(chain[way] == d)
                def _():
                    for c in DUE[d][point]:
                        wall_copy(way, wait_g[way], c).wait_recv()
                        if d < NZ - 1:
                            wall_copy(way, send_g[way], c).start()
                        for i in range(1, nx):
                            across_copy(way, c, i).start()

    def pump_first():
        for way in range(2):

            @pl.when(chain[way] == NZ - 1)
            def _():
                for c in range(PARTS):
                    wall_copy(way, zh, c).start()

    def pump_last():
        for way in range(2):
            for c in range(PARTS):
                for i in range(1, nx):
                    across_got(way, c, i)

    for i in range(1, NY):
        keep_copy(i).start()
    for i in range(1, NY):
        cut_copy(i).start()
    own_w.wait()
    pump_first()

    for i in range(1, NY):
        o = in_row(i)
        remote(keeps.at[o], keeps.at[o], keep_s.at[o], keep_r.at[o], at(pos, col)).wait_recv()
        remote(cut.at[o], got.at[o], cut_s.at[o], cut_r.at[o], at(pos, col)).wait_recv()
    run = [jnp.zeros((sr, MEM), F32) for _ in range(4)]
    decayed = [jnp.ones((1, MEM), F32) for _ in range(2)]
    decayed_at = []
    for b in range(NY):
        decayed_at.append(list(decayed))
        for h in range(2):
            kb = keeps[b, h : h + 1, :]
            for hl in (2 * h, 2 * h + 1):
                inner[b, hl] = run[hl]
                run[hl] = run[hl] * kb + got[b, hl].astype(F32)
            decayed[h] = decayed[h] * kb

    def tiles():
        t = 0
        for hl in range(4):
            for dh in range(dh_n):
                for jh in range(2):
                    yield t // tps, t % tps, hl, slice(dh * SUB, (dh + 1) * SUB), slice(jh * LANES, (jh + 1) * LANES)
                    t += 1

    for owner, slot, hl, ds_, js in tiles():
        tot[owner, slot, 0] = run[hl][ds_, js]
        tot[owner, slot, 1] = jnp.broadcast_to(decayed[hl // 2][:, js], (SUB, LANES))
    rows_in[r] = tot[r]

    def tot_copy(i):
        to = in_rows(i)
        return remote(tot.at[to], rows_in.at[r], tot_s.at[to], tot_r.at[r], at(to * NY + y, col))

    for i in range(1, nr):
        tot_copy(i).start()

    def halo_got(k):
        remote(halo.at[0], halo.at[k], halo_s.at[k - 1], halo_r.at[k], at(pos, col)).wait_recv()

    halo_copy(0, 2).start()
    pump(0)

    for i in range(1, nr):
        o = in_rows(i)
        remote(tot.at[o], rows_in.at[o], tot_s.at[o], tot_r.at[o], at(pos, col)).wait_recv()
    for slot in range(tps):
        e = jnp.zeros((SUB, LANES), F32)
        for rr in range(nr):
            ent[rr, slot] = e
            e = e * rows_in[rr, slot, 1] + rows_in[rr, slot, 0]
    ent_in[r] = ent[r]

    def ent_copy(i):
        to = in_rows(i)
        return remote(ent.at[to], ent_in.at[r], ent_s.at[to], ent_r.at[r], at(to * NY + y, col))

    for i in range(1, nr):
        ent_copy(i).start()

    pump(1)

    for i in range(1, nr):
        o = in_rows(i)
        remote(ent.at[o], ent_in.at[o], ent_s.at[o], ent_r.at[o], at(pos, col)).wait_recv()
    for owner, slot, hl, ds_, js in tiles():
        e = ent_in[owner, slot]
        for b in range(NY):
            whole = inner[b, hl, ds_, js] + e * decayed_at[b][hl // 2][:, js]
            inner[b, hl, ds_, js] = whole
    for b in range(NY):
        for hl in range(4):
            back[b, hl] = inner[b, hl].astype(BF16)
    back_in[y] = back[y]

    def back_copy(i):
        to = in_row(i)
        return remote(back.at[to], back_in.at[y], back_s.at[to], back_r.at[y], at(r * NY + to, col))

    for i in range(1, NY):
        back_copy(i).start()

    pump(2)

    for i in range(1, NY):
        o = in_row(i)
        remote(back.at[o], back_in.at[o], back_s.at[o], back_r.at[o], at(pos, col)).wait_recv()
    read = []
    for h in range(2):
        kh = keep2[h : h + 1, :]
        state = []
        for layer in range(2):
            hl = 2 * h + layer
            entering = jnp.concatenate([back_in[s, hl] for s in range(NY)], 0).astype(F32)
            state.append(entering * kh + upd[hl])
        fast_first = (m1_ref[h].astype(F32) + state[0]).astype(BF16)
        fast_second = (m2_ref[h].astype(F32).T + state[1]).astype(BF16)
        zq = dot(q_ref[:, h * HD : (h + 1) * HD], fast_first, 1, 0)
        recall = (zq * jax.nn.sigmoid(zq)).astype(BF16)
        read.append(dot(recall, fast_second, 1, 1).astype(BF16))
    reads[zh] = jnp.concatenate(read, 1)

    def read_copy(g):
        return remote(
            reads.at[zh], reads.at[zh], read_s.at[g], read_r.at[zh], at(pos, lax.rem(col + 2 * g, n_col))
        )

    for g in range(1, groups):
        read_copy(g).start()

    halo_got(2)
    halo_copy(2, 2).start()
    halo_copy(2, 1).start()
    halo_copy(0, 1).start()
    pump_last()
    for g in range(1, groups):
        o = lax.rem(zh + g, groups)
        remote(reads.at[o], reads.at[o], read_s.at[g], read_r.at[o], at(pos, col)).wait_recv()
    left = jnp.concatenate([reads[g] for g in range(groups)], 1)

    def part_copy(c):
        return remote(part.at[c], part_in.at[c], part_s.at[c], part_r.at[c], at(pos, sibling))

    for c in range(n_out):
        cs = slice(c * OUT_COLS, (c + 1) * OUT_COLS)
        right = jnp.concatenate([wall[g, :, cs] for g in range(groups)], 0)
        part[c] = dot(left, right, 1, 0).astype(BF16)
        part_copy(c).start()
    halo_got(1)
    halo_got(3)
    halo_got(4)
    scale = 1.0 / math.sqrt(HD)
    causal = lax.broadcasted_iota(jnp.int32, (HD, HD), 1) <= lax.broadcasted_iota(jnp.int32, (HD, HD), 0)
    clear = jnp.ones((1, HD), F32)
    clear_at = []
    for k in range(1, WMAX + 1):
        clear = clear * (1.0 - halo[k - 1, 2 * HD : 2 * HD + 16, 0:HD].astype(F32)[0:1])
        clear_at.append(clear * jnp.where(pos >= k, 1.0, 0.0))
    for h in range(2):
        cols = slice(h * HD, (h + 1) * HD)
        qh = q_ref[:, cols]
        s = [jnp.where(causal, dot(qh, halo[0, 0:HD, cols], 1, 1) * scale, -1e30)]
        for k in range(1, WMAX + 1):
            ok = clear_at[k - 1] * jnp.where(win_ref[h] >= k, 1.0, 0.0)
            s.append(jnp.where(ok > 0.5, dot(qh, halo[k, 0:HD, cols], 1, 1) * scale, -1e30))
        s = jnp.concatenate(s, 1)
        top = jnp.max(s, axis=1, keepdims=True)
        e = jnp.exp(s - top)
        w = (e / jnp.sum(e, axis=1, keepdims=True)).astype(BF16)
        vals = jnp.concatenate([halo[k, HD : 2 * HD, cols] for k in range(WMAX + 1)], 0)
        att_ref[:, cols] = dot(w, vals, 1, 0).astype(BF16)

    for c in range(n_out):
        cs = slice(c * OUT_COLS, (c + 1) * OUT_COLS)
        part_copy(c).wait_recv()
        out_ref[:, cs] = (part[c].astype(F32) + part_in[c].astype(F32)).astype(BF16)

    for i in range(1, NY):
        keep_copy(i).wait_send()
        cut_copy(i).wait_send()
        back_copy(i).wait_send()
    for i in range(1, nr):
        tot_copy(i).wait_send()
        ent_copy(i).wait_send()
    for k in (0, 2):
        for ahead in (1, 2):
            halo_copy(k, ahead).wait_send()
    for g in range(1, groups):
        read_copy(g).wait_send()
    for way in range(2):
        for c in range(PARTS):
            wall_copy(way, send_g[way], c).wait_send()
            for i in range(1, nx):
                across_copy(way, c, i).wait_send()
    for c in range(n_out):
        part_copy(c).wait_send()


def solution(mesh):
    n_stretch, n_col = mesh.shape["stretch"], mesh.shape["col"]
    nr, groups, sr = n_stretch // NY, n_col // 2, HD // NY
    tps = 4 * (sr // SUB) * 2 // nr

    def shards(queries, keys, values, memory_first, memory_second_weight, out_weight, decay, boundary, win_blocks):
        d = out_weight.shape[1]
        hbm = pl.BlockSpec(memory_space=pltpu.HBM)
        vmem = pl.BlockSpec(memory_space=pltpu.VMEM)
        dma = pltpu.SemaphoreType.DMA
        return tuple(
            pl.pallas_call(
                functools.partial(kernel, n_stretch, n_col),
                out_shape=(
                    jax.ShapeDtypeStruct((HD, 2 * HD), BF16),
                    jax.ShapeDtypeStruct((HD, d), BF16),
                ),
                in_specs=[hbm] * 8 + [pl.BlockSpec(memory_space=pltpu.SMEM)],
                out_specs=(vmem, vmem),
                scratch_shapes=[
                    pltpu.VMEM((HD, 2 * HD), BF16),
                    pltpu.VMEM((2, HD, MEM), BF16),
                    pltpu.VMEM((2, MEM, HD), BF16),
                    pltpu.VMEM((1, 2, MEM), F32),
                    pltpu.SMEM((2,), jnp.int32),
                    pltpu.VMEM((WMAX + 1, 2 * HD + 16, 2 * HD), BF16),
                    pltpu.VMEM((NY, SUB, MEM), F32),
                    pltpu.VMEM((4, HD, MEM), F32),
                    pltpu.VMEM((NY, 4, sr, MEM), BF16),
                    pltpu.VMEM((NY, 4, sr, MEM), BF16),
                    pltpu.VMEM((NY, 4, sr, MEM), F32),
                    pltpu.VMEM((nr, tps, 2, SUB, LANES), F32),
                    pltpu.VMEM((nr, tps, 2, SUB, LANES), F32),
                    pltpu.VMEM((nr, tps, SUB, LANES), F32),
                    pltpu.VMEM((nr, tps, SUB, LANES), F32),
                    pltpu.VMEM((NY, 4, sr, MEM), BF16),
                    pltpu.VMEM((NY, 4, sr, MEM), BF16),
                    pltpu.VMEM((groups, 2 * HD, d), BF16),
                    pltpu.VMEM((groups, HD, 2 * HD), BF16),
                    pltpu.VMEM((d // OUT_COLS, HD, OUT_COLS), BF16),
                    pltpu.VMEM((d // OUT_COLS, HD, OUT_COLS), BF16),
                    dma((7,)),
                    dma((WMAX + 1,)),
                    dma((WMAX + 1,)),
                    dma((NY,)),
                    dma((NY,)),
                    dma((NY,)),
                    dma((NY,)),
                    dma((nr,)),
                    dma((nr,)),
                    dma((nr,)),
                    dma((nr,)),
                    dma((NY,)),
                    dma((NY,)),
                    dma((PARTS,)),
                    dma((PARTS,)),
                    dma((PARTS,)),
                    dma((PARTS,)),
                    dma((2, PARTS, nr // NZ)),
                    dma((2, PARTS, nr // NZ)),
                    dma,
                    dma((groups,)),
                    dma((groups,)),
                    dma((d // OUT_COLS,)),
                    dma((d // OUT_COLS,)),
                ],
                compiler_params=pltpu.CompilerParams(
                    collective_id=0, has_side_effects=True, vmem_limit_bytes=48 * 2**20
                ),
            )(
                *(
                    pltpu.with_memory_space_constraint(x, pltpu.HBM)
                    for x in (
                        queries,
                        keys,
                        values,
                        memory_first,
                        memory_second_weight,
                        out_weight,
                        decay,
                        win_blocks,
                    )
                ),
                boundary,
            )
        )

    placed = (
        P("stretch", "col"),
        P("stretch", "col"),
        P("stretch", "col"),
        P("col", None, None),
        P("col", None, None),
        P("col", None),
        P("stretch", "col", None),
        P("stretch"),
        P("col"),
    )
    return jax.shard_map(
        shards,
        mesh=mesh,
        in_specs=placed,
        out_specs=(P("stretch", "col"), P("stretch", None)),
        check_vma=False,
    )
```
